512 devices in a mesh: src: 16 (over x, z_hi, core), dst: 32 (over y, z_lo).
Axes of the slice: x: 4, y: 8, z: 8 (z_hi: 2, z_lo: 4; z = z_hi * 4 + z_lo), core: 2. Of those that a mesh axis runs over, the one named last changes fastest.
Arguments:
- source_emb: float32 [65536, 400], P(('src', 'dst')), may hold values from -4.5 to 4.5
- dest_emb: float32 [65536, 400], P(('src', 'dst')), may hold values from -4.5 to 4.5
- source_acc: float32 [65536], P(('src', 'dst')), may hold values from 0.01 to 1
- dest_acc: float32 [65536], P(('src', 'dst')), may hold values from 0.01 to 1
- relations: float32 [256, 400], replicated, may hold values from -1 to 1
- rel_acc: float32 [256], replicated, may hold values from 1 to 100
- src_ids: int32 [16, 32, 2, 1000], P('src', 'dst'), may hold values from 0 to 127
- dst_ids: int32 [16, 32, 2, 1000], P('src', 'dst'), may hold values from 0 to 127
- rel_ids: int32 [16, 32, 2, 1000], P('src', 'dst'), may hold values from 0 to 255, as said below
- neg_ids: int32 [16, 32, 2, 1000], P('src', 'dst'), may hold values from 0 to 127
- counts: int32 [16, 32, 2], P('src', 'dst'), may hold values from 125 to 1000
Outputs:
- new_source: float32 [65536, 400], P(('src', 'dst'))
- new_dest: float32 [65536, 400], P(('src', 'dst'))
- new_source_acc: float32 [65536], P(('src', 'dst'))
- new_dest_acc: float32 [65536], P(('src', 'dst'))
- new_relations: float32 [256, 400], replicated
- new_rel_acc: float32 [256], replicated
The draws below stay inside these ranges and needn't reach their ends.
Inputs may be any that keep to these rules, and one draw needn't show every extreme that they name: `rel_ids`: the relation types of bucket (i, j, s) lie in 8 r to 8 r + 15, taken mod 256, with r = i * 32 + j.
All inputs are finite; a program needn't handle non-finite values.
Results may differ from the reference program's by a relative error of at most 0.0035.
Values may be sent and summed in bfloat16 or wider, within the bound.
A program may use at most 64 MiB of HBM per device.

```python
import math
import jax
import jax.numpy as jnp
from jax import lax

EMB = 400
BLK = 128
REL = 256
GROUP = 1000
NEG = 1000
STEPS = 2
ROWS = 65536
N_SRC = 16
N_DST = 32


def entity_table(key):
    keys = jax.random.split(key, 5)
    return jnp.clip(0.5 * jax.random.normal(keys[4], (ROWS, EMB), jnp.float32), -3.0, 3.0)


def draw_source_emb(key, part):
    key = jax.random.fold_in(key, 1)
    return entity_table(key)


def draw_dest_emb(key, part):
    key = jax.random.fold_in(key, 2)
    return entity_table(key)


def draw_relations(key, part):
    key = jax.random.fold_in(key, 3)
    first = jax.random.fold_in(key, 0)
    return jnp.clip(0.25 * jax.random.normal(first, (REL, EMB), jnp.float32), -1.0, 1.0)


def draw_counts(key, part):
    key = jax.random.fold_in(key, 5)
    lowest = GROUP // 8
    picks = jax.random.randint(key, (N_SRC * N_DST * STEPS,), 0, 32, jnp.int32)
    picks = picks.at[0].set(31).at[1].set(0)
    cubes = picks * picks * picks
    return (lowest + (GROUP - lowest) * cubes // 29791).reshape(N_SRC, N_DST, STEPS).astype(jnp.int32)


def draw_rel_ids(key, part):
    key = jax.random.fold_in(key, 7)
    device_rank = jnp.arange(N_SRC, dtype=jnp.int32)[:, None] * N_DST + jnp.arange(N_DST, dtype=jnp.int32)[None, :]
    offsets = jax.random.randint(key, (N_SRC, N_DST, STEPS, GROUP), 0, 16, jnp.int32)
    offsets = offsets.at[:, :, :, 0].set(15).at[:, :, :, 1].set(0)
    return ((device_rank[:, :, None, None] * 8 + offsets) % REL).astype(jnp.int32)


def plant(array, stream_key, smallest, top_value):
    longest = array.shape.index(max(array.shape))
    spots = []
    for shift in (0, 1):
        where = [jax.random.randint(jax.random.fold_in(stream_key, axis), (), 0, length) for axis, length in enumerate(array.shape)]
        where[longest] = (where[longest] + shift) % array.shape[longest]
        spots.append(tuple(where))
    return array.at[spots[0]].set(smallest).at[spots[1]].set(top_value)


def level_of(rng, shape, shards, low, largest):
    gain, own = 1.0, jax.random.fold_in(rng, 6)
    for position, parts in shards:
        heights = jnp.exp(jax.random.uniform(jax.random.fold_in(own, position), (parts,), jnp.float32, low / len(shards), largest / len(shards)))
        gain = gain * jnp.repeat(heights, shape[position] // parts).reshape([-1 if axis == position else 1 for axis in range(len(shape))])
    return gain


def setup_inputs(seed: int = 0) -> dict:
    seeds = jax.random.split(jax.random.key(seed), 12)
    source_emb = draw_source_emb(jax.random.fold_in(seeds[11], 71), 0)
    dest_emb = draw_dest_emb(jax.random.fold_in(seeds[11], 71), 0)
    source_acc = jnp.clip(jnp.exp(math.log(1.0) - 4.6051702 * jax.random.uniform(seeds[2], (ROWS,), jnp.float32) ** level_of(seeds[2], (ROWS,), ((0, 512),), -0.2, 0.2)), 0.01, 1.0)
    dest_acc = jnp.clip(jnp.exp(math.log(1.0) - 4.6051702 * jax.random.uniform(seeds[3], (ROWS,), jnp.float32) ** level_of(seeds[3], (ROWS,), ((0, 512),), -0.2, 0.2)), 0.01, 1.0)
    relations = draw_relations(jax.random.fold_in(seeds[11], 71), 0)
    rel_acc = jnp.clip(jnp.exp(jax.random.uniform(seeds[5], (REL,), jnp.float32, math.log(1.0), math.log(100.0))), 1.0, 100.0)
    src_ids = plant(jax.random.randint(seeds[6], (N_SRC, N_DST, STEPS, GROUP), 0, BLK), jax.random.fold_in(seeds[6], 1), 0, BLK - 1).astype(jnp.int32)
    dst_ids = plant(jax.random.randint(seeds[7], (N_SRC, N_DST, STEPS, GROUP), 0, BLK), jax.random.fold_in(seeds[7], 1), 0, BLK - 1).astype(jnp.int32)
    rel_ids = draw_rel_ids(jax.random.fold_in(seeds[11], 71), 0)
    neg_ids = plant(jax.random.randint(seeds[9], (N_SRC, N_DST, STEPS, NEG), 0, BLK), jax.random.fold_in(seeds[9], 1), 0, BLK - 1).astype(jnp.int32)
    counts = draw_counts(jax.random.fold_in(seeds[11], 71), 0)
    return dict(source_emb=source_emb, dest_emb=dest_emb, source_acc=source_acc, dest_acc=dest_acc, relations=relations, rel_acc=rel_acc, src_ids=src_ids, dst_ids=dst_ids, rel_ids=rel_ids, neg_ids=neg_ids, counts=counts)


learn_rate = 0.1

def product(left, right, dims):
    return lax.dot_general(left, right, (dims, ((), ())), preferred_element_type=jnp.float32)

def bucket_terms(src_block, dst_block, rel_table, src_index, dst_index, rel_index, neg_index, live_count):
    half_width = src_block.shape[1] // 2
    source_rows = jnp.take(src_block, src_index, axis=0).astype(jnp.float32)
    target_rows = jnp.take(dst_block, dst_index, axis=0).astype(jnp.float32)
    relation_rows = jnp.take(rel_table, rel_index, axis=0).astype(jnp.float32)
    src_real = source_rows[:, :half_width]
    src_imag = source_rows[:, half_width:]
    rel_real = relation_rows[:, :half_width]
    rel_imag = relation_rows[:, half_width:]
    queries = jnp.concatenate([src_real * rel_real - src_imag * rel_imag, src_real * rel_imag + src_imag * rel_real], axis=1)
    positive = lax.optimization_barrier(jnp.sum(queries * target_rows, axis=1))
    query_low = queries.astype(jnp.bfloat16)
    negatives = jnp.take(dst_block, neg_index, axis=0)
    scores = product(query_low, negatives, ((1,), (1,)))
    peak_score = jnp.maximum(lax.optimization_barrier(jnp.max(scores, axis=1)), positive)
    pos_weight = jnp.exp(positive - peak_score)
    neg_weight = jnp.exp(scores - peak_score[:, None])
    partition = pos_weight + lax.optimization_barrier(jnp.sum(neg_weight, axis=1))
    valid_mask = (jnp.arange(scores.shape[0]) < live_count).astype(jnp.float32)
    pos_coeff = valid_mask * (pos_weight / partition - 1.0)
    neg_coeff = ((valid_mask / partition)[:, None] * neg_weight).astype(jnp.bfloat16)
    query_grad = pos_coeff[:, None] * target_rows + product(neg_coeff, negatives, ((1,), (0,)))
    negative_grad = product(neg_coeff, query_low, ((0,), (0,)))
    positive_grad = pos_coeff[:, None] * queries
    grad_real = query_grad[:, :half_width]
    grad_imag = query_grad[:, half_width:]
    source_grad = jnp.concatenate([grad_real * rel_real + grad_imag * rel_imag, grad_imag * rel_real - grad_real * rel_imag], axis=1)
    relation_grad = jnp.concatenate([grad_real * src_real + grad_imag * src_imag, grad_imag * src_real - grad_real * src_imag], axis=1)
    return (source_grad, positive_grad, negative_grad, relation_grad)

def row_adagrad(table, accum, grad):
    new_accum = accum + lax.optimization_barrier(jnp.mean(grad * grad, axis=1))
    return (table - learn_rate * grad / jnp.sqrt(new_accum)[:, None], new_accum)

def reference(source_emb, dest_emb, source_acc, dest_acc, relations, rel_acc, src_ids, dst_ids, rel_ids, neg_ids, counts):
    src_low = source_emb.astype(jnp.bfloat16).reshape(N_SRC * N_DST, BLK, EMB)
    dst_low = dest_emb.astype(jnp.bfloat16).reshape(N_SRC * N_DST, BLK, EMB)
    rel_low = relations.astype(jnp.bfloat16)
    src_flat = src_ids.reshape(-1, GROUP)
    dst_flat = dst_ids.reshape(-1, GROUP)
    rel_flat = rel_ids.reshape(-1, GROUP)
    neg_flat = neg_ids.reshape(-1, NEG)
    count_flat = counts.reshape(-1)

    def visit(carried, bucket_index):
        source_total, dest_total, relation_total = carried
        grid_cell = bucket_index // STEPS
        step_index = bucket_index % STEPS
        grid_row = grid_cell // N_DST
        grid_col = grid_cell % N_DST
        src_place = grid_row * N_DST + (grid_col - step_index) % N_DST
        dst_place = (grid_row - step_index) % N_SRC * N_DST + grid_col
        source_grad, positive_grad, negative_grad, relation_grad = bucket_terms(src_low[src_place], dst_low[dst_place], rel_low, src_flat[bucket_index], dst_flat[bucket_index], rel_flat[bucket_index], neg_flat[bucket_index], count_flat[bucket_index])
        source_term = jax.ops.segment_sum(source_grad, src_flat[bucket_index], num_segments=BLK)
        target_index = jnp.concatenate([dst_flat[bucket_index], neg_flat[bucket_index]])
        target_term = jax.ops.segment_sum(jnp.concatenate([positive_grad, negative_grad], axis=0), target_index, num_segments=BLK)
        relation_term = jax.ops.segment_sum(relation_grad, rel_flat[bucket_index], num_segments=REL)
        source_total = source_total.at[src_place].add(source_term)
        dest_total = dest_total.at[dst_place].add(target_term)
        return ((source_total, dest_total, relation_total + relation_term), None)
    start_state = (jnp.zeros((N_SRC * N_DST, BLK, EMB), jnp.float32), jnp.zeros((N_SRC * N_DST, BLK, EMB), jnp.float32), jnp.zeros((REL, EMB), jnp.float32))
    finals, unused = lax.scan(visit, start_state, jnp.arange(N_SRC * N_DST * STEPS, dtype=jnp.int32))
    grad_source = finals[0].reshape(ROWS, EMB)
    grad_dest = finals[1].reshape(ROWS, EMB)
    new_source, new_source_acc = row_adagrad(source_emb, source_acc, grad_source)
    new_dest, new_dest_acc = row_adagrad(dest_emb, dest_acc, grad_dest)
    new_relations, new_rel_acc = row_adagrad(relations, rel_acc, finals[2])
    return (new_source, new_dest, new_source_acc, new_dest_acc, new_relations, new_rel_acc)
```

```python
import functools

import jax
import jax.numpy as jnp
from jax import lax
from jax.experimental import pallas as pl
from jax.experimental.pallas import tpu as pltpu
from jax.sharding import PartitionSpec as P

MESH = pl.DeviceIdType.MESH
F32 = jnp.float32
BF16 = jnp.bfloat16
learn_rate = 0.1

ZH, ZL, NC = 2, 4, 2
LANES = 128
CHUNK = 256
ABSENT = -1e30


def split2(value):
    high = value.astype(BF16)
    low = (value - high.astype(F32)).astype(BF16)
    return high, low


def nn(left, right):
    return jnp.dot(left, right, preferred_element_type=F32)


def nt(left, right):
    return lax.dot_general(left, right, (((1,), (1,)), ((), ())), preferred_element_type=F32)


def kernel(
    NX,
    NY,
    counts,
    source_emb,
    dest_emb,
    source_acc,
    dest_acc,
    relations,
    rel_acc,
    src_ids,
    dst_ids,
    rel_ids,
    neg_ids,
    new_source,
    new_dest,
    new_source_acc,
    new_dest_acc,
    new_relations,
    new_rel_acc,
    ids,
    src_t,
    dst_t,
    dst_n,
    rel_t,
    count_b,
    query_s,
    weight_s,
    grad_s,
    rel_sum,
    src_sum,
    dst_sum,
    back_out,
    back_in,
    turn,
    acc_b,
    part,
    part_in,
    mine,
    column,
    full,
    x_send,
    x_recv,
    b_send,
    b_recv,
    s1_send,
    s1_recv,
    s2_send,
    s2_recv,
    s3_send,
    s3_recv,
    s4_send,
    s4_recv,
    s5_send,
    s5_recv,
):
    emb = source_emb.shape[1]
    half = emb // 2
    slots = src_ids.shape[1]
    chunks = pl.cdiv(slots, CHUNK)
    tail = slots - (chunks - 1) * CHUNK
    n_src, n_dst = NX * ZH * NC, NY * ZL
    rel_count = relations.shape[0]
    blocks = [(b * LANES, min(LANES, emb - b * LANES)) for b in range(NX)]

    i = lax.axis_index("src")
    j = lax.axis_index("dst")
    x, zh, c = i // (ZH * NC), (i // NC) % ZH, i % NC
    y, zl = j // ZL, j % ZL

    def place(x, zh, c, y, zl):
        return ((x * ZH + zh) * NC + c, y * ZL + zl)

    def wrap(value, size):
        return lax.rem(value, size)

    ring_next = ((i, wrap(j + 1, n_dst)), (wrap(i + 1, n_src), j))
    ring_prev = ((i, wrap(j + n_dst - 1, n_dst)), (wrap(i + n_src - 1, n_src), j))
    s1_steps = [(dx, dc) for dx in range(NX) for dc in range(NC) if dx or dc]
    s1_peers = [place(wrap(x + dx, NX), zh, wrap(c + dc, NC), y, zl) for dx, dc in s1_steps]
    s2_steps = [(dh, dl, dc) for dh in range(ZH) for dl in range(ZL) for dc in range(NC)]
    special = jnp.logical_and(zl == ZL - 1, c == 1)
    far_y = jnp.where(special, wrap(y + 1, NY), y)

    def s2_peer(step, at_y):
        dh, dl, dc = step
        return place(x, wrap(zh + dh, ZH), wrap(c + dc, NC), at_y, wrap(zl + dl, ZL))

    s3_peers = [place(x, zh, c, wrap(y + dy, NY), zl) for dy in range(1, NY)]
    s4_peers = [place(wrap(x + dx, NX), zh, c, y, zl) for dx in range(1, NX)]
    sibling = place(x, zh, 1 - c, y, zl)

    barrier = pltpu.get_barrier_semaphore()
    greeted = list(ring_next) + list(ring_prev) + s1_peers + s3_peers
    greeted += [s2_peer(step, y) for step in s2_steps[1:]]
    expected = len(greeted)
    before_y = wrap(y + NY - 1, NY)
    greeted += [place(x, h, 1, before_y, ZL - 1) for h in range(ZH)]
    for peer in greeted:
        pl.semaphore_signal(barrier, inc=1, device_id=peer, device_id_type=MESH)

    def turned(block):
        width = block.shape[1]
        if width < LANES:
            block = jnp.concatenate([block, jnp.zeros((block.shape[0], LANES - width), F32)], axis=1)
        return block.T[:width]

    for start, width in blocks:
        src_t[0, start : start + width, :] = turned(source_emb[:, start : start + width]).astype(BF16)
        dst_t[0, start : start + width, :] = turned(dest_emb[:, start : start + width]).astype(BF16)
    dst_n[0, :, :] = dest_emb[...].astype(BF16)

    pl.semaphore_wait(barrier, jnp.where(special, expected + ZH * ZL * NC, expected))

    def remote(src, dst, send, recv, peer):
        return pltpu.make_async_remote_copy(
            src_ref=src, dst_ref=dst, send_sem=send, recv_sem=recv, device_id=peer, device_id_type=MESH
        )

    give_src = remote(src_t.at[0], src_t.at[1], x_send.at[0], x_recv.at[0], ring_next[0])
    give_dst = remote(dst_t.at[0], dst_t.at[1], x_send.at[1], x_recv.at[1], ring_next[1])
    give_src.start()
    give_dst.start()

    first = pl.multiple_of(j * 8, 8)
    second = pl.multiple_of(wrap(j + 1, n_dst) * 8, 8)
    rel_rows = jnp.concatenate(
        [relations[pl.ds(first, 8), :], relations[pl.ds(second, 8), :], jnp.zeros((LANES - 16, emb), F32)], axis=0
    )
    for start, width in blocks:
        rel_t[start : start + width, :] = turned(rel_rows[:, start : start + width]).astype(BF16)

    ids[...] = jnp.full(ids.shape, -1, jnp.int32)
    for s in range(2):
        for n, table in enumerate((src_ids, dst_ids, rel_ids, neg_ids)):
            for q in range(chunks):
                width = CHUNK if q < chunks - 1 else tail
                row = table[s : s + 1, q * CHUNK : q * CHUNK + width]
                if n == 2:
                    row = jnp.bitwise_and(row - 8 * j, rel_count - 1)
                ids[s * chunks + q, n : n + 1, 0:width] = row

    iota = lax.broadcasted_iota(jnp.int32, (LANES, CHUNK), 0)
    lane = lax.broadcasted_iota(jnp.int32, (1, CHUNK), 1)

    for s in range(2):
        seen = jnp.zeros((LANES, CHUNK), F32)
        for q in range(chunks):
            seen = seen + jnp.where(iota == ids[s * chunks + q, 3:4, :], 1.0, 0.0)
        count_b[s] = jnp.broadcast_to(jnp.sum(seen, axis=1, keepdims=True), (LANES, CHUNK))

    rel_sum[...] = jnp.zeros(rel_sum.shape, F32)
    src_sum[...] = jnp.zeros(src_sum.shape, F32)
    dst_sum[...] = jnp.zeros(dst_sum.shape, F32)
    turn[...] = jnp.zeros(turn.shape, F32)
    wide = min(LANES, rel_count)
    for b in range(rel_count // wide):
        row = rel_acc[0:1, b * wide : (b + 1) * wide]
        acc_b[b * wide : (b + 1) * wide, :] = jnp.broadcast_to(row, (LANES, wide)).T

    def first_pass(s):
        live_count = counts[s]

        def body(local, carry):
            q = s * chunks + local
            rows = ids[q]
            one_src = jnp.where(iota == rows[0:1], 1.0, 0.0).astype(BF16)
            hit_dst = iota == rows[1:2]
            one_rel = jnp.where(iota == rows[2:3], 1.0, 0.0).astype(BF16)
            a = nn(src_t[s], one_src)
            r = nn(rel_t[...], one_rel)
            a_re, a_im, r_re, r_im = a[:half], a[half:], r[:half], r[half:]
            query = jnp.concatenate([a_re * r_re - a_im * r_im, a_re * r_im + a_im * r_re], axis=0)
            query_high, query_low = split2(query)
            scores = nn(dst_n[s], query_high)
            rest = nn(dst_n[s], query_low)
            positive = jnp.sum(jnp.where(hit_dst, scores + rest, 0.0), axis=0, keepdims=True)
            seen = count_b[s]
            scores = jnp.where(seen > 0.0, scores, ABSENT)
            peak = jnp.maximum(jnp.max(scores, axis=0, keepdims=True), positive)
            pos_weight = jnp.exp(positive - peak)
            neg_weight = jnp.exp(scores - peak)
            partition = pos_weight + jnp.sum(neg_weight * seen, axis=0, keepdims=True)
            live = jnp.where(lane + local * CHUNK < live_count, 1.0, 0.0)
            pos_coeff = live * (pos_weight / partition - 1.0)
            neg_coeff = (neg_weight * (live / partition)).astype(BF16).astype(F32)
            pos_part = jnp.where(hit_dst, pos_coeff, 0.0)
            weight_high, weight_low = split2(neg_coeff * seen + pos_part)
            query_s[q, 0] = query_high
            query_s[q, 1] = query_low
            weight_s[q, 0] = weight_high
            weight_s[q, 1] = weight_low
            weight_s[q, 2] = pos_part.astype(BF16)
            table = dst_t[s]
            g = nn(
                jnp.concatenate([table, table], axis=1),
                jnp.concatenate([weight_high, weight_low], axis=0),
            )
            g_re, g_im = g[:half], g[half:]
            rel_grad = jnp.concatenate([g_re * a_re + g_im * a_im, g_im * a_re - g_re * a_im], axis=0)
            rel_high, rel_low = split2(rel_grad)
            rel_sum[0:emb, :] += nt(rel_high, one_rel) + nt(rel_low, one_rel)
            src_grad = jnp.concatenate([g_re * r_re + g_im * r_im, g_im * r_re - g_re * r_im], axis=0)
            src_high, src_low = split2(src_grad)
            grad_s[q, 0] = src_high
            grad_s[q, 1] = src_low
            return carry

        lax.fori_loop(0, chunks, body, 0)

    def second_pass(s):
        def body(local, carry):
            q = s * chunks + local
            rows = ids[q]
            one_src = jnp.where(iota == rows[0:1], 1.0, 0.0).astype(BF16)
            src_sum[s] += nt(grad_s[q, 0], one_src) + nt(grad_s[q, 1], one_src)
            dst_sum[s] += (
                nt(query_s[q, 0], weight_s[q, 0])
                + nt(query_s[q, 0], weight_s[q, 1])
                + nt(query_s[q, 1], weight_s[q, 2])
            )
            return carry

        lax.fori_loop(0, chunks, body, 0)

    first_pass(0)
    give_src.wait()
    give_dst.wait()
    for start, width in blocks:
        block = dst_t[1, start : start + width, :].astype(F32)
        if width < LANES:
            block = jnp.concatenate([block, jnp.zeros((LANES - width, LANES), F32)], axis=0)
        dst_n[1, :, start : start + width] = block.T[:, :width].astype(BF16)
    first_pass(1)

    for b in range(NX):
        block = rel_sum[b * LANES : (b + 1) * LANES, :].T
        for rows in range(NC):
            part[b, rows] = block[8 * rows : 8 * rows + 8, :]
    s1 = [
        remote(
            part.at[wrap(x + dx, NX), wrap(c + dc, NC)],
            part_in.at[n],
            s1_send.at[n],
            s1_recv.at[n],
            s1_peers[n],
        )
        for n, (dx, dc) in enumerate(s1_steps)
    ]
    for copy in s1:
        copy.start()

    second_pass(1)
    back_out[0] = src_sum[1].astype(BF16)
    back_out[1] = dst_sum[1].astype(BF16)
    back = [remote(back_out.at[n], back_in.at[n], b_send.at[n], b_recv.at[n], ring_prev[n]) for n in range(2)]
    for copy in back:
        copy.start()

    tile = part[x, c]
    for n, copy in enumerate(s1):
        copy.wait()
        tile = tile + part_in[n]
    mine[...] = tile

    s2 = [
        remote(mine, column.at[zh, zl, c], s2_send.at[n], s2_recv.at[n], s2_peer(step, far_y))
        for n, step in enumerate(s2_steps)
    ]
    for copy in s2[1:]:
        copy.start()

    @pl.when(special)
    def _():
        s2[0].start()

    @pl.when(jnp.logical_not(special))
    def _():
        column[zh, zl, c] = mine[...]

    second_pass(0)
    for copy in s2[1:]:
        copy.wait()

    @pl.when(special)
    def _():
        s2[0].wait()

    firsts = [column[0, l, 0] + column[1, l, 0] for l in range(ZL)]
    lasts = [column[0, l, 1] + column[1, l, 1] for l in range(ZL)]
    whole = [firsts[l] + lasts[(l + ZL - 1) % ZL] for l in range(ZL)]
    for n in range(2):
        full[x, y, c, n] = jnp.where(c == 0, whole[n], whole[2 + n])
    order = sorted(range(NY), key=lambda dy: (min(dy, NY - dy), dy))
    s3 = {
        dy: remote(full.at[x, y, c], full.at[x, y, c], s3_send.at[dy], s3_recv.at[dy], s3_peers[dy - 1])
        for dy in order
        if dy
    }
    for dy in order[1:]:
        s3[dy].start()

    def s4_copies(dy):
        at = full.at[x, wrap(y + NY - dy, NY), c]
        return [
            remote(at, at, s4_send.at[dy, n], s4_recv.at[dy, n], s4_peers[n]) for n in range(NX - 1)
        ]

    def s5_copy(dy):
        at = full.at[:, wrap(y + NY - dy, NY), c]
        return remote(at, at, s5_send.at[dy], s5_recv.at[dy], sibling)

    s4 = {dy: s4_copies(dy) for dy in order}
    s5 = {dy: s5_copy(dy) for dy in order}
    for copy in s4[0]:
        copy.start()

    def update(n, sums, table, acc, out, new_acc):
        back[n].wait()
        total = sums[0] + back_in[n].astype(F32)
        accum = acc[...] + jnp.sum(total * total, axis=0, keepdims=True) * (1.0 / emb)
        new_acc[...] = accum
        turn[0:emb, :] = total * (learn_rate / jnp.sqrt(accum))
        for b, (start, width) in enumerate(blocks):
            step = turn[b * LANES : (b + 1) * LANES, :].T
            out[:, start : start + width] = table[:, start : start + width] - step[:, :width]

    update(0, src_sum, source_emb, source_acc, new_source, new_source_acc)
    update(1, dst_sum, dest_emb, dest_acc, new_dest, new_dest_acc)

    def to_sibling(dy):
        for copy in s4[dy]:
            copy.wait_recv()
        s5[dy].start()

    lag = 3
    for n, dy in enumerate(order):
        if dy:
            s3[dy].wait_recv()
            for copy in s4[dy]:
                copy.start()
        if n >= lag:
            to_sibling(order[n - lag])
    for dy in order[max(0, NY - lag) :]:
        to_sibling(dy)
    for dy in order:
        s5[dy].wait_recv()

    tiles = [full[b].reshape(rel_count, LANES) for b in range(NX)]
    squares = tiles[0] * tiles[0]
    for tile in tiles[1:]:
        squares = squares + tile * tile
    accum = acc_b[...] + jnp.sum(squares, axis=1, keepdims=True) * (1.0 / emb)
    scale = learn_rate / jnp.sqrt(accum)
    for b, (start, width) in enumerate(blocks):
        step = tiles[b] * scale
        new_relations[:, start : start + width] = relations[:, start : start + width] - step[:, :width]
    for b in range(rel_count // wide):
        block = accum[b * wide : (b + 1) * wide, :].T
        new_rel_acc[0:1, b * wide : (b + 1) * wide] = block[0:1, :]

    for dy in order:
        if dy:
            s3[dy].wait_send()
        for copy in s4[dy]:
            copy.wait_send()
        s5[dy].wait_send()


def solution(mesh):
    n_src, n_dst = mesh.shape["src"], mesh.shape["dst"]
    NX, NY = n_src // (ZH * NC), n_dst // ZL

    def shards(
        source_emb,
        dest_emb,
        source_acc,
        dest_acc,
        relations,
        rel_acc,
        src_ids,
        dst_ids,
        rel_ids,
        neg_ids,
        counts,
    ):
        rows, emb = source_emb.shape
        rel_count = relations.shape[0]
        slots = src_ids.shape[3]
        chunks = pl.cdiv(slots, CHUNK)
        vmem = pl.BlockSpec(memory_space=pltpu.VMEM)
        smem = pl.BlockSpec(memory_space=pltpu.SMEM)
        dma = pltpu.SemaphoreType.DMA
        outs = pl.pallas_call(
            functools.partial(kernel, NX, NY),
            out_shape=(
                jax.ShapeDtypeStruct((rows, emb), F32),
                jax.ShapeDtypeStruct((rows, emb), F32),
                jax.ShapeDtypeStruct((1, rows), F32),
                jax.ShapeDtypeStruct((1, rows), F32),
                jax.ShapeDtypeStruct((rel_count, emb), F32),
                jax.ShapeDtypeStruct((1, rel_count), F32),
            ),
            in_specs=[smem] + [vmem] * 10,
            out_specs=[vmem] * 6,
            scratch_shapes=[
                pltpu.VMEM((2 * chunks, 4, CHUNK), jnp.int32),
                pltpu.VMEM((2, emb, LANES), BF16),
                pltpu.VMEM((2, emb, LANES), BF16),
                pltpu.VMEM((2, LANES, emb), BF16),
                pltpu.VMEM((emb, LANES), BF16),
                pltpu.VMEM((2, LANES, CHUNK), F32),
                pltpu.VMEM((2 * chunks, 2, emb, CHUNK), BF16),
                pltpu.VMEM((2 * chunks, 3, LANES, CHUNK), BF16),
                pltpu.VMEM((2 * chunks, 2, emb, CHUNK), BF16),
                pltpu.VMEM((NX * LANES, LANES), F32),
                pltpu.VMEM((2, emb, LANES), F32),
                pltpu.VMEM((2, emb, LANES), F32),
                pltpu.VMEM((2, emb, LANES), BF16),
                pltpu.VMEM((2, emb, LANES), BF16),
                pltpu.VMEM((NX * LANES, LANES), F32),
                pltpu.VMEM((rel_count, LANES), F32),
                pltpu.VMEM((NX, NC, 8, LANES), F32),
                pltpu.VMEM((NX * NC - 1, 8, LANES), F32),
                pltpu.VMEM((8, LANES), F32),
                pltpu.VMEM((ZH, ZL, NC, 8, LANES), F32),
                pltpu.VMEM((NX, NY, NC, ZL // NC, 8, LANES), F32),
                dma((2,)),
                dma((2,)),
                dma((2,)),
                dma((2,)),
                dma((NX * NC - 1,)),
                dma((NX * NC - 1,)),
                dma((ZH * ZL * NC,)),
                dma((ZH * ZL * NC,)),
                dma((NY,)),
                dma((NY,)),
                dma((NY, NX - 1)),
                dma((NY, NX - 1)),
                dma((NY,)),
                dma((NY,)),
            ],
            compiler_params=pltpu.CompilerParams(
                collective_id=0, has_side_effects=True, vmem_limit_bytes=40 * 2**20
            ),
            cost_estimate=pl.CostEstimate(flops=4 * 10**9, bytes_accessed=3 * 10**6, transcendentals=3 * 10**5),
            name="bucket_round",
        )(
            counts.reshape(2),
            source_emb,
            dest_emb,
            source_acc.reshape(1, rows),
            dest_acc.reshape(1, rows),
            relations,
            rel_acc.reshape(1, rel_count),
            src_ids.reshape(2, slots),
            dst_ids.reshape(2, slots),
            rel_ids.reshape(2, slots),
            neg_ids.reshape(2, slots),
        )
        new_source, new_dest, new_source_acc, new_dest_acc, new_relations, new_rel_acc = outs
        return (
            new_source,
            new_dest,
            new_source_acc.reshape(rows),
            new_dest_acc.reshape(rows),
            new_relations,
            new_rel_acc.reshape(rel_count),
        )

    rows_spec = P(("src", "dst"), None)
    row_spec = P(("src", "dst"))
    ids_spec = P("src", "dst", None, None)
    return jax.shard_map(
        shards,
        mesh=mesh,
        in_specs=(rows_spec, rows_spec, row_spec, row_spec, P(), P())
        + (ids_spec,) * 4
        + (P("src", "dst", None),),
        out_specs=(rows_spec, rows_spec, row_spec, row_spec, P(), P()),
        check_vma=False,
    )
```

```python
import functools

import jax
import jax.numpy as jnp
from jax import lax
from jax.experimental import pallas as pl
from jax.experimental.pallas import tpu as pltpu
from jax.sharding import PartitionSpec as P

MESH = pl.DeviceIdType.MESH
F32 = jnp.float32
BF16 = jnp.bfloat16
learn_rate = 0.1

ZH, ZL, NC = 2, 4, 2
LANES = 128
CHUNK = 256
ABSENT = -1e30


def split2(value):
    high = value.astype(BF16)
    low = (value - high.astype(F32)).astype(BF16)
    return high, low


def nn(left, right):
    return jnp.dot(left, right, preferred_element_type=F32)


def nt(left, right):
    return lax.dot_general(left, right, (((1,), (1,)), ((), ())), preferred_element_type=F32)


def kernel(
    NX,
    NY,
    counts_hbm,
    source_emb_hbm,
    dest_emb_hbm,
    source_acc_hbm,
    dest_acc_hbm,
    relations_hbm,
    rel_acc_hbm,
    src_ids_hbm,
    dst_ids_hbm,
    rel_ids_hbm,
    neg_ids_hbm,
    new_source,
    new_dest,
    new_source_acc,
    new_dest_acc,
    new_relations,
    new_rel_acc,
    counts,
    source_emb,
    dest_emb,
    source_acc,
    dest_acc,
    relations,
    rel_acc,
    src_ids,
    dst_ids,
    rel_ids,
    neg_ids,
    ids,
    src_t,
    dst_t,
    dst_n,
    rel_t,
    count_b,
    query_s,
    weight_s,
    grad_s,
    rel_sum,
    src_sum,
    dst_sum,
    back_out,
    back_in,
    part,
    part_in,
    mine,
    column,
    full,
    in_sem,
    x_send,
    x_recv,
    b_send,
    b_recv,
    s1_send,
    s1_recv,
    s2_send,
    s2_recv,
    s3_send,
    s3_recv,
    s4_send,
    s4_recv,
    s5_send,
    s5_recv,
):
    loads = [
        pltpu.make_async_copy(src, dst, in_sem.at[n])
        for n, (src, dst) in enumerate(
            (
                (counts_hbm, counts),
                (rel_ids_hbm, rel_ids),
                (src_ids_hbm, src_ids),
                (dst_ids_hbm, dst_ids),
                (neg_ids_hbm, neg_ids),
                (source_emb_hbm, source_emb),
                (dest_emb_hbm, dest_emb),
                (relations_hbm, relations),
                (source_acc_hbm, source_acc),
                (dest_acc_hbm, dest_acc),
                (rel_acc_hbm, rel_acc),
            )
        )
    ]
    for load in loads:
        load.start()

    emb = source_emb.shape[0]
    half = emb // 2
    slots = src_ids.shape[1]
    chunks = pl.cdiv(slots, CHUNK)
    tail = slots - (chunks - 1) * CHUNK
    n_src, n_dst = NX * ZH * NC, NY * ZL
    rel_count = relations.shape[1]
    blocks = [(b * LANES, min(LANES, emb - b * LANES)) for b in range(NX)]

    i = lax.axis_index("src")
    j = lax.axis_index("dst")
    x, zh, c = i // (ZH * NC), jnp.bitwise_and(i // NC, ZH - 1), jnp.bitwise_and(i, NC - 1)
    y, zl = j // ZL, jnp.bitwise_and(j, ZL - 1)

    def place(x, zh, c, y, zl):
        return ((x * ZH + zh) * NC + c, y * ZL + zl)

    def wrap(value, size):
        return jnp.bitwise_and(value, size - 1)

    i_up, i_down = wrap(i + 1, n_src), wrap(i + n_src - 1, n_src)
    j_up, j_down = wrap(j + 1, n_dst), wrap(j + n_dst - 1, n_dst)
    ring = [(i_down, j), (i_up, j), (i_down, j_up), (i_up, j_down)]
    s1_steps = [(dx, dc) for dx in range(NX) for dc in range(NC) if dx or dc]
    s1_peers = [place(wrap(x + dx, NX), zh, wrap(c + dc, NC), y, zl) for dx, dc in s1_steps]
    s2_steps = [(dh, dl, dc) for dh in range(ZH) for dl in range(ZL) for dc in range(NC)]
    special = jnp.logical_and(zl == ZL - 1, c == 1)
    far_y = jnp.where(special, wrap(y + 1, NY), y)

    def s2_peer(step, at_y):
        dh, dl, dc = step
        return place(x, wrap(zh + dh, ZH), wrap(c + dc, NC), at_y, wrap(zl + dl, ZL))

    s3_peers = [place(x, zh, c, wrap(y + dy, NY), zl) for dy in range(1, NY)]
    s4_peers = [place(wrap(x + dx, NX), zh, c, y, zl) for dx in range(1, NX)]
    sibling = place(x, zh, 1 - c, y, zl)

    barrier = pltpu.get_barrier_semaphore()
    greeted = ring + s1_peers + s3_peers
    greeted += [s2_peer(step, y) for step in s2_steps[1:]]
    expected = len(greeted)
    before_y = wrap(y + NY - 1, NY)
    greeted += [place(x, h, 1, before_y, ZL - 1) for h in range(ZH)]
    for peer in greeted:
        pl.semaphore_signal(barrier, inc=1, device_id=peer, device_id_type=MESH)

    def remote(src, dst, send, recv, peer):
        return pltpu.make_async_remote_copy(
            src_ref=src, dst_ref=dst, send_sem=send, recv_sem=recv, device_id=peer, device_id_type=MESH
        )

    lane = lax.broadcasted_iota(jnp.int32, (1, CHUNK), 1)
    for to in (0, 2):
        ids[to] = jnp.full(ids.shape[1:], -1, jnp.int32)
    for load in loads[:5]:
        load.wait()
    for s, to in ((1, 2), (0, 0)):
        live_count = counts[s]
        for n, table in enumerate((src_ids, dst_ids, rel_ids, neg_ids)):
            for q in range(chunks):
                width = CHUNK if q < chunks - 1 else tail
                row = table[s : s + 1, q * CHUNK : q * CHUNK + width]
                if n == 2:
                    row = jnp.bitwise_and(row - 8 * j, rel_count - 1)
                    row = jnp.where(lane[:, :width] + q * CHUNK < live_count, row, -1)
                ids[to, q, n : n + 1, 0:width] = row
    loads[5].wait()
    src_t[0] = source_emb[...].astype(BF16)

    pl.semaphore_wait(barrier, jnp.where(special, expected + ZH * ZL * NC, expected))
    give_ids = remote(ids.at[2], ids.at[1], x_send.at[0], x_recv.at[0], ring[0])
    give_src = remote(src_t.at[0], src_t.at[1], x_send.at[1], x_recv.at[1], ring[2])
    give_ids.start()
    give_src.start()
    for load in loads[6:]:
        load.wait()

    dst_t[...] = dest_emb[...].astype(BF16)
    for start, width in blocks:
        block = dest_emb[start : start + width, :]
        if width < LANES:
            block = jnp.concatenate([block, jnp.zeros((LANES - width, LANES), F32)], axis=0)
        dst_n[:, start : start + width] = block.T[:, :width].astype(BF16)

    row = lax.broadcasted_iota(jnp.int32, (rel_count, LANES), 0)
    spot = lax.broadcasted_iota(jnp.int32, (rel_count, LANES), 1)
    chosen = jnp.logical_and(row == jnp.bitwise_and(spot + 8 * j, rel_count - 1), spot < 16)
    rel_t[...] = nn(relations[...].astype(BF16), jnp.where(chosen, 1.0, 0.0).astype(BF16)).astype(BF16)

    iota = lax.broadcasted_iota(jnp.int32, (LANES, CHUNK), 0)

    def count_rows(s):
        seen = jnp.zeros((LANES, CHUNK), F32)
        for q in range(chunks):
            seen = seen + jnp.where(iota == ids[s, q, 3:4, :], 1.0, 0.0)
        count_b[s] = jnp.broadcast_to(jnp.sum(seen, axis=1, keepdims=True), (LANES, CHUNK))

    rel_sum[...] = jnp.zeros(rel_sum.shape, F32)
    src_sum[...] = jnp.zeros(src_sum.shape, F32)
    dst_sum[...] = jnp.zeros(dst_sum.shape, F32)

    def first_pass(s):
        def body(local, carry):
            q = s * chunks + local
            rows = ids[s, local]
            one_src = jnp.where(iota == rows[0:1], 1.0, 0.0).astype(BF16)
            hit_dst = iota == rows[1:2]
            one_rel = jnp.where(iota == rows[2:3], 1.0, 0.0).astype(BF16)
            a = nn(src_t[s], one_src)
            r = nn(rel_t[...], one_rel)
            a_re, a_im, r_re, r_im = a[:half], a[half:], r[:half], r[half:]
            query = jnp.concatenate([a_re * r_re - a_im * r_im, a_re * r_im + a_im * r_re], axis=0)
            query_high, query_low = split2(query)
            scores = nn(dst_n[...], query_high)
            rest = nn(dst_n[...], query_low)
            positive = jnp.sum(jnp.where(hit_dst, scores + rest, 0.0), axis=0, keepdims=True)
            seen = count_b[s]
            scores = jnp.where(seen > 0.0, scores, ABSENT)
            peak = jnp.maximum(jnp.max(scores, axis=0, keepdims=True), positive)
            pos_weight = jnp.exp(positive - peak)
            neg_weight = jnp.exp(scores - peak)
            partition = pos_weight + jnp.sum(neg_weight * seen, axis=0, keepdims=True)
            pos_coeff = pos_weight / partition - 1.0
            neg_coeff = (neg_weight * (1.0 / partition)).astype(BF16).astype(F32)
            pos_part = jnp.where(hit_dst, pos_coeff, 0.0)
            weight_high, weight_low = split2(neg_coeff * seen + pos_part)
            query_s[q, 0] = query_high
            query_s[q, 1] = query_low
            weight_s[q, 0] = weight_high
            weight_s[q, 1] = weight_low
            weight_s[q, 2] = pos_part.astype(BF16)
            table = dst_t[...]
            g = nn(
                jnp.concatenate([table, table], axis=1),
                jnp.concatenate([weight_high, weight_low], axis=0),
            )
            g_re, g_im = g[:half], g[half:]
            rel_grad = jnp.concatenate([g_re * a_re + g_im * a_im, g_im * a_re - g_re * a_im], axis=0)
            rel_high, rel_low = split2(rel_grad)
            rel_sum[0:emb, :] += nt(rel_high, one_rel) + nt(rel_low, one_rel)
            src_grad = jnp.concatenate([g_re * r_re + g_im * r_im, g_im * r_re - g_re * r_im], axis=0)
            src_high, src_low = split2(src_grad)
            grad_s[q, 0] = src_high
            grad_s[q, 1] = src_low
            return carry

        lax.fori_loop(0, chunks, body, 0)

    def second_pass(s):
        def body(local, carry):
            q = s * chunks + local
            rows = ids[s, local]
            one_src = jnp.where(iota == rows[0:1], 1.0, 0.0).astype(BF16)
            src_sum[s] += nt(grad_s[q, 0], one_src) + nt(grad_s[q, 1], one_src)
            dst_sum[...] += (
                nt(query_s[q, 0], weight_s[q, 0])
                + nt(query_s[q, 0], weight_s[q, 1])
                + nt(query_s[q, 1], weight_s[q, 2])
            )
            return carry

        lax.fori_loop(0, chunks, body, 0)

    count_rows(0)
    first_pass(0)
    second_pass(0)
    give_ids.wait()
    give_src.wait()
    count_rows(1)
    first_pass(1)

    for b in range(NX):
        block = rel_sum[b * LANES : (b + 1) * LANES, :].T
        for rows in range(NC):
            part[b, rows] = block[8 * rows : 8 * rows + 8, :]
    s1 = [
        remote(
            part.at[wrap(x + dx, NX), wrap(c + dc, NC)],
            part_in.at[n],
            s1_send.at[n],
            s1_recv.at[n],
            s1_peers[n],
        )
        for n, (dx, dc) in enumerate(s1_steps)
    ]
    for copy in s1:
        copy.start()

    second_pass(1)
    back_out[...] = src_sum[1].astype(BF16)
    back = remote(back_out, back_in, b_send.at[0], b_recv.at[0], ring[3])
    back.start()

    tile = part[x, c]
    for n, copy in enumerate(s1):
        copy.wait()
        tile = tile + part_in[n]
    mine[...] = tile

    s2 = [
        remote(mine, column.at[zh, zl, c], s2_send.at[n], s2_recv.at[n], s2_peer(step, far_y))
        for n, step in enumerate(s2_steps)
    ]
    for copy in s2[1:]:
        copy.start()

    @pl.when(special)
    def _():
        s2[0].start()

    @pl.when(jnp.logical_not(special))
    def _():
        column[zh, zl, c] = mine[...]

    for copy in s2[1:]:
        copy.wait()

    @pl.when(special)
    def _():
        s2[0].wait()

    firsts = [column[0, l, 0] + column[1, l, 0] for l in range(ZL)]
    lasts = [column[0, l, 1] + column[1, l, 1] for l in range(ZL)]
    whole = [firsts[l] + lasts[(l + ZL - 1) % ZL] for l in range(ZL)]
    for n in range(2):
        full[x, y, c, n] = jnp.where(c == 0, whole[n], whole[2 + n])
    order = sorted(range(NY), key=lambda dy: (min(dy, NY - dy), dy))
    s3 = {
        dy: remote(full.at[x, y, c], full.at[x, y, c], s3_send.at[dy], s3_recv.at[dy], s3_peers[dy - 1])
        for dy in order
        if dy
    }
    for dy in order[1:]:
        s3[dy].start()

    def s4_copies(dy):
        at = full.at[x, wrap(y + NY - dy, NY), c]
        return [
            remote(at, at, s4_send.at[dy, n], s4_recv.at[dy, n], s4_peers[n]) for n in range(NX - 1)
        ]

    def s5_copy(dy):
        at = full.at[:, wrap(y + NY - dy, NY), c]
        return remote(at, at, s5_send.at[dy], s5_recv.at[dy], sibling)

    s4 = {dy: s4_copies(dy) for dy in order}
    s5 = {dy: s5_copy(dy) for dy in order}
    for copy in s4[0]:
        copy.start()

    def update(total, table, acc, out, new_acc):
        accum = acc[...] + jnp.sum(total * total, axis=0, keepdims=True) * (1.0 / emb)
        new_acc[...] = accum
        out[...] = table[...] - total * (learn_rate / jnp.sqrt(accum))

    update(dst_sum[...], dest_emb, dest_acc, new_dest, new_dest_acc)
    back.wait()
    update(src_sum[0] + back_in[...].astype(F32), source_emb, source_acc, new_source, new_source_acc)

    def to_sibling(dy):
        for copy in s4[dy]:
            copy.wait_recv()
        s5[dy].start()

    lag = 3
    for n, dy in enumerate(order):
        if dy:
            s3[dy].wait_recv()
            for copy in s4[dy]:
                copy.start()
        if n >= lag:
            to_sibling(order[n - lag])
    for dy in order[max(0, NY - lag) :]:
        to_sibling(dy)
    for dy in order:
        s5[dy].wait_recv()

    wide = min(LANES, rel_count)
    for h in range(rel_count // wide):
        at = slice(h * wide, (h + 1) * wide)
        tiles = [full[b].reshape(rel_count, LANES)[at].T[:width] for b, (start, width) in enumerate(blocks)]
        squares = sum(jnp.sum(tile * tile, axis=0, keepdims=True) for tile in tiles)
        accum = rel_acc[0:1, at] + squares * (1.0 / emb)
        new_rel_acc[0:1, at] = accum
        scale = learn_rate / jnp.sqrt(accum)
        for tile, (start, width) in zip(tiles, blocks):
            new_relations[start : start + width, at] = relations[start : start + width, at] - tile * scale

    for dy in order:
        if dy:
            s3[dy].wait_send()
        for copy in s4[dy]:
            copy.wait_send()
        s5[dy].wait_send()


def write_out(*refs):
    count = (len(refs) - 1) // 2
    sem = refs[-1]
    copies = [pltpu.make_async_copy(refs[n], refs[count + n], sem.at[n]) for n in range(count)]
    for copy in copies:
        copy.start()
    for copy in copies:
        copy.wait()


def solution(mesh):
    n_src, n_dst = mesh.shape["src"], mesh.shape["dst"]
    NX, NY = n_src // (ZH * NC), n_dst // ZL

    def shards(
        source_emb,
        dest_emb,
        source_acc,
        dest_acc,
        relations,
        rel_acc,
        src_ids,
        dst_ids,
        rel_ids,
        neg_ids,
        counts,
    ):
        rows, emb = source_emb.shape
        rel_count = relations.shape[0]
        slots = src_ids.shape[3]
        chunks = pl.cdiv(slots, CHUNK)
        hbm = pl.BlockSpec(memory_space=pl.ANY)
        vmem = pl.BlockSpec(memory_space=pltpu.VMEM)
        dma = pltpu.SemaphoreType.DMA
        outs = pl.pallas_call(
            functools.partial(kernel, NX, NY),
            out_shape=(
                pltpu.VMEM((emb, rows), F32),
                pltpu.VMEM((emb, rows), F32),
                pltpu.VMEM((1, rows), F32),
                pltpu.VMEM((1, rows), F32),
                pltpu.VMEM((emb, rel_count), F32),
                pltpu.VMEM((1, rel_count), F32),
            ),
            in_specs=[hbm] * 11,
            out_specs=[vmem] * 6,
            scratch_shapes=[
                pltpu.SMEM((2,), jnp.int32),
                pltpu.VMEM((emb, rows), F32),
                pltpu.VMEM((emb, rows), F32),
                pltpu.VMEM((1, rows), F32),
                pltpu.VMEM((1, rows), F32),
                pltpu.VMEM((emb, rel_count), F32),
                pltpu.VMEM((1, rel_count), F32),
                pltpu.VMEM((2, slots), jnp.int32),
                pltpu.VMEM((2, slots), jnp.int32),
                pltpu.VMEM((2, slots), jnp.int32),
                pltpu.VMEM((2, slots), jnp.int32),
                pltpu.VMEM((3, chunks, 4, CHUNK), jnp.int32),
                pltpu.VMEM((2, emb, LANES), BF16),
                pltpu.VMEM((emb, LANES), BF16),
                pltpu.VMEM((LANES, emb), BF16),
                pltpu.VMEM((emb, LANES), BF16),
                pltpu.VMEM((2, LANES, CHUNK), F32),
                pltpu.VMEM((2 * chunks, 2, emb, CHUNK), BF16),
                pltpu.VMEM((2 * chunks, 3, LANES, CHUNK), BF16),
                pltpu.VMEM((2 * chunks, 2, emb, CHUNK), BF16),
                pltpu.VMEM((NX * LANES, LANES), F32),
                pltpu.VMEM((2, emb, LANES), F32),
                pltpu.VMEM((emb, LANES), F32),
                pltpu.VMEM((emb, LANES), BF16),
                pltpu.VMEM((emb, LANES), BF16),
                pltpu.VMEM((NX, NC, 8, LANES), F32),
                pltpu.VMEM((NX * NC - 1, 8, LANES), F32),
                pltpu.VMEM((8, LANES), F32),
                pltpu.VMEM((ZH, ZL, NC, 8, LANES), F32),
                pltpu.VMEM((NX, NY, NC, ZL // NC, 8, LANES), F32),
                dma((11,)),
                dma((2,)),
                dma((2,)),
                dma((1,)),
                dma((1,)),
                dma((NX * NC - 1,)),
                dma((NX * NC - 1,)),
                dma((ZH * ZL * NC,)),
                dma((ZH * ZL * NC,)),
                dma((NY,)),
                dma((NY,)),
                dma((NY, NX - 1)),
                dma((NY, NX - 1)),
                dma((NY,)),
                dma((NY,)),
            ],
            compiler_params=pltpu.CompilerParams(
                collective_id=0, has_side_effects=True, vmem_limit_bytes=40 * 2**20
            ),
            cost_estimate=pl.CostEstimate(flops=4 * 10**9, bytes_accessed=3 * 10**6, transcendentals=3 * 10**5),
            name="bucket_round",
        )(
            *(
                pltpu.with_memory_space_constraint(value, pltpu.HBM)
                for value in (
                    counts.reshape(2),
                    source_emb.T,
                    dest_emb.T,
                    source_acc.reshape(1, rows),
                    dest_acc.reshape(1, rows),
                    relations.T,
                    rel_acc.reshape(1, rel_count),
                    src_ids.reshape(2, slots),
                    dst_ids.reshape(2, slots),
                    rel_ids.reshape(2, slots),
                    neg_ids.reshape(2, slots),
                )
            )
        )
        outs = pl.pallas_call(
            write_out,
            out_shape=tuple(pltpu.HBM(out.shape, out.dtype) for out in outs),
            in_specs=[vmem] * 6,
            out_specs=[hbm] * 6,
            scratch_shapes=[dma((6,))],
            name="write_out",
        )(*(pltpu.with_memory_space_constraint(out, pltpu.VMEM) for out in outs))
        new_source, new_dest, new_source_acc, new_dest_acc, new_relations, new_rel_acc = outs
        return (
            new_source.T,
            new_dest.T,
            new_source_acc.reshape(rows),
            new_dest_acc.reshape(rows),
            new_relations.T,
            new_rel_acc.reshape(rel_count),
        )

    rows_spec = P(("src", "dst"), None)
    row_spec = P(("src", "dst"))
    ids_spec = P("src", "dst", None, None)
    return jax.shard_map(
        shards,
        mesh=mesh,
        in_specs=(rows_spec, rows_spec, row_spec, row_spec, P(), P())
        + (ids_spec,) * 4
        + (P("src", "dst", None),),
        out_specs=(rows_spec, rows_spec, row_spec, row_spec, P(), P()),
        check_vma=False,
    )
```

```python
import functools

import jax
import jax.numpy as jnp
from jax import lax
from jax.experimental import pallas as pl
from jax.experimental.pallas import tpu as pltpu
from jax.sharding import PartitionSpec as P

MESH = pl.DeviceIdType.MESH
F32 = jnp.float32
BF16 = jnp.bfloat16
learn_rate = 0.1

ZH, ZL, NC = 2, 4, 2
LANES = 128
CHUNK = 256
ABSENT = -1e30


def split2(value):
    high = value.astype(BF16)
    low = (value - high.astype(F32)).astype(BF16)
    return high, low


def nn(left, right):
    return jnp.dot(left, right, preferred_element_type=F32)


def nt(left, right):
    return lax.dot_general(left, right, (((1,), (1,)), ((), ())), preferred_element_type=F32)


def kernel(
    NX,
    NY,
    counts_hbm,
    source_emb_hbm,
    dest_emb_hbm,
    source_acc_hbm,
    dest_acc_hbm,
    relations_hbm,
    rel_acc_hbm,
    src_ids_hbm,
    dst_ids_hbm,
    rel_ids_hbm,
    neg_ids_hbm,
    new_source,
    new_dest,
    new_source_acc,
    new_dest_acc,
    new_relations,
    new_rel_acc,
    counts,
    source_emb,
    dest_emb,
    source_acc,
    dest_acc,
    relations,
    rel_acc,
    src_ids,
    dst_ids,
    rel_ids,
    neg_ids,
    ids,
    src_t,
    dst_t,
    dst_n,
    rel_t,
    count_b,
    query_s,
    weight_s,
    grad_s,
    rel_sum,
    src_sum,
    dst_sum,
    back_out,
    back_in,
    part,
    part_in,
    mine,
    column,
    full,
    in_sem,
    x_send,
    x_recv,
    b_send,
    b_recv,
    s1_send,
    s1_recv,
    s2_send,
    s2_recv,
    s3_send,
    s3_recv,
    s4_send,
    s4_recv,
    s5_send,
    s5_recv,
):
    loads = [
        pltpu.make_async_copy(src, dst, in_sem.at[n])
        for n, (src, dst) in enumerate(
            (
                (counts_hbm, counts),
                (rel_ids_hbm, rel_ids),
                (src_ids_hbm, src_ids),
                (dst_ids_hbm, dst_ids),
                (neg_ids_hbm, neg_ids),
                (source_emb_hbm, source_emb),
                (dest_emb_hbm, dest_emb),
                (relations_hbm, relations),
                (source_acc_hbm, source_acc),
                (dest_acc_hbm, dest_acc),
                (rel_acc_hbm, rel_acc),
            )
        )
    ]

    emb = source_emb.shape[0]
    half = emb // 2
    slots = src_ids.shape[1]
    chunks = pl.cdiv(slots, CHUNK)
    tail = slots - (chunks - 1) * CHUNK
    n_src, n_dst = NX * ZH * NC, NY * ZL
    rel_count = relations.shape[1]
    blocks = [(b * LANES, min(LANES, emb - b * LANES)) for b in range(NX)]

    i = lax.axis_index("src")
    j = lax.axis_index("dst")
    x, zh, c = i // (ZH * NC), jnp.bitwise_and(i // NC, ZH - 1), jnp.bitwise_and(i, NC - 1)
    y, zl = j // ZL, jnp.bitwise_and(j, ZL - 1)

    def place(x, zh, c, y, zl):
        return ((x * ZH + zh) * NC + c, y * ZL + zl)

    def wrap(value, size):
        return jnp.bitwise_and(value, size - 1)

    i_up, i_down = wrap(i + 1, n_src), wrap(i + n_src - 1, n_src)
    j_up, j_down = wrap(j + 1, n_dst), wrap(j + n_dst - 1, n_dst)
    ring = [(i_down, j), (i_up, j), (i_down, j_up), (i_up, j_down)]
    s1_steps = [(dx, dc) for dx in range(NX) for dc in range(NC) if dx or dc]
    s1_peers = [place(wrap(x + dx, NX), zh, wrap(c + dc, NC), y, zl) for dx, dc in s1_steps]
    s2_steps = [(dh, dl, dc) for dh in range(ZH) for dl in range(ZL) for dc in range(NC)]
    special = jnp.logical_and(zl == ZL - 1, c == 1)
    far_y = jnp.where(special, wrap(y + 1, NY), y)

    def s2_peer(step, at_y):
        dh, dl, dc = step
        return place(x, wrap(zh + dh, ZH), wrap(c + dc, NC), at_y, wrap(zl + dl, ZL))

    s3_peers = [place(x, zh, c, wrap(y + dy, NY), zl) for dy in range(1, NY)]
    s4_peers = [place(wrap(x + dx, NX), zh, c, y, zl) for dx in range(1, NX)]
    sibling = place(x, zh, 1 - c, y, zl)

    barrier = pltpu.get_barrier_semaphore()
    greeted = ring + s1_peers + s3_peers
    greeted += [s2_peer(step, y) for step in s2_steps[1:]]
    expected = len(greeted)
    before_y = wrap(y + NY - 1, NY)
    greeted += [place(x, h, 1, before_y, ZL - 1) for h in range(ZH)]
    for n, peer in enumerate(greeted):
        pl.semaphore_signal(barrier, inc=1, device_id=peer, device_id_type=MESH)
        if n == len(ring) - 1:
            for load in loads:
                load.start()

    def remote(src, dst, send, recv, peer):
        return pltpu.make_async_remote_copy(
            src_ref=src, dst_ref=dst, send_sem=send, recv_sem=recv, device_id=peer, device_id_type=MESH
        )

    lane = lax.broadcasted_iota(jnp.int32, (1, CHUNK), 1)
    for to in (0, 2):
        ids[to] = jnp.full(ids.shape[1:], -1, jnp.int32)
    for load in loads[:5]:
        load.wait()
    for s, to in ((1, 2), (0, 0)):
        live_count = counts[s]
        for n, table in enumerate((src_ids, dst_ids, rel_ids, neg_ids)):
            for q in range(chunks):
                width = CHUNK if q < chunks - 1 else tail
                row = table[s : s + 1, q * CHUNK : q * CHUNK + width]
                if n == 2:
                    row = jnp.bitwise_and(row - 8 * j, rel_count - 1)
                    row = jnp.where(lane[:, :width] + q * CHUNK < live_count, row, -1)
                ids[to, q, n : n + 1, 0:width] = row
    loads[5].wait()
    src_t[0] = source_emb[...].astype(BF16)

    pl.semaphore_wait(barrier, jnp.where(special, expected + ZH * ZL * NC, expected))
    give_ids = remote(ids.at[2], ids.at[1], x_send.at[0], x_recv.at[0], ring[0])
    give_src = remote(src_t.at[0], src_t.at[1], x_send.at[1], x_recv.at[1], ring[2])
    give_ids.start()
    give_src.start()
    for load in loads[6:]:
        load.wait()

    dst_t[...] = dest_emb[...].astype(BF16)
    for start, width in blocks:
        block = dest_emb[start : start + width, :]
        if width < LANES:
            block = jnp.concatenate([block, jnp.zeros((LANES - width, LANES), F32)], axis=0)
        dst_n[:, start : start + width] = block.T[:, :width].astype(BF16)

    row = lax.broadcasted_iota(jnp.int32, (rel_count, LANES), 0)
    spot = lax.broadcasted_iota(jnp.int32, (rel_count, LANES), 1)
    chosen = jnp.logical_and(row == jnp.bitwise_and(spot + 8 * j, rel_count - 1), spot < 16)
    rel_t[...] = nn(relations[...].astype(BF16), jnp.where(chosen, 1.0, 0.0).astype(BF16)).astype(BF16)

    iota = lax.broadcasted_iota(jnp.int32, (LANES, CHUNK), 0)

    def count_rows(s):
        seen = jnp.zeros((LANES, CHUNK), F32)
        for q in range(chunks):
            seen = seen + jnp.where(iota == ids[s, q, 3:4, :], 1.0, 0.0)
        count_b[s] = jnp.broadcast_to(jnp.sum(seen, axis=1, keepdims=True), (LANES, CHUNK))

    rel_sum[...] = jnp.zeros(rel_sum.shape, F32)
    src_sum[...] = jnp.zeros(src_sum.shape, F32)
    dst_sum[...] = jnp.zeros(dst_sum.shape, F32)

    def first_pass(s):
        def body(local, carry):
            q = s * chunks + local
            rows = ids[s, local]
            one_src = jnp.where(iota == rows[0:1], 1.0, 0.0).astype(BF16)
            hit_dst = iota == rows[1:2]
            one_rel = jnp.where(iota == rows[2:3], 1.0, 0.0).astype(BF16)
            a = nn(src_t[s], one_src)
            r = nn(rel_t[...], one_rel)
            a_re, a_im, r_re, r_im = a[:half], a[half:], r[:half], r[half:]
            query = jnp.concatenate([a_re * r_re - a_im * r_im, a_re * r_im + a_im * r_re], axis=0)
            query_high, query_low = split2(query)
            scores = nn(dst_n[...], query_high)
            rest = nn(dst_n[...], query_low)
            positive = jnp.sum(jnp.where(hit_dst, scores + rest, 0.0), axis=0, keepdims=True)
            seen = count_b[s]
            scores = jnp.where(seen > 0.0, scores, ABSENT)
            peak = jnp.maximum(jnp.max(scores, axis=0, keepdims=True), positive)
            pos_weight = jnp.exp(positive - peak)
            neg_weight = jnp.exp(scores - peak)
            partition = pos_weight + jnp.sum(neg_weight * seen, axis=0, keepdims=True)
            pos_coeff = pos_weight / partition - 1.0
            neg_coeff = (neg_weight * (1.0 / partition)).astype(BF16).astype(F32)
            pos_part = jnp.where(hit_dst, pos_coeff, 0.0)
            weight_high, weight_low = split2(neg_coeff * seen + pos_part)
            query_s[q, 0] = query_high
            query_s[q, 1] = query_low
            weight_s[q, 0] = weight_high
            weight_s[q, 1] = weight_low
            weight_s[q, 2] = pos_part.astype(BF16)
            table = dst_t[...]
            g = nn(
                jnp.concatenate([table, table], axis=1),
                jnp.concatenate([weight_high, weight_low], axis=0),
            )
            g_re, g_im = g[:half], g[half:]
            rel_grad = jnp.concatenate([g_re * a_re + g_im * a_im, g_im * a_re - g_re * a_im], axis=0)
            rel_high, rel_low = split2(rel_grad)
            rel_sum[0:emb, :] += nt(rel_high, one_rel) + nt(rel_low, one_rel)
            src_grad = jnp.concatenate([g_re * r_re + g_im * r_im, g_im * r_re - g_re * r_im], axis=0)
            src_high, src_low = split2(src_grad)
            grad_s[q, 0] = src_high
            grad_s[q, 1] = src_low
            return carry

        lax.fori_loop(0, chunks, body, 0, unroll=True)

    def second_pass(s):
        def body(local, carry):
            q = s * chunks + local
            rows = ids[s, local]
            one_src = jnp.where(iota == rows[0:1], 1.0, 0.0).astype(BF16)
            src_sum[s] += nt(grad_s[q, 0], one_src) + nt(grad_s[q, 1], one_src)
            dst_sum[...] += (
                nt(query_s[q, 0], weight_s[q, 0])
                + nt(query_s[q, 0], weight_s[q, 1])
                + nt(query_s[q, 1], weight_s[q, 2])
            )
            return carry

        lax.fori_loop(0, chunks, body, 0, unroll=True)

    count_rows(0)
    first_pass(0)
    second_pass(0)
    give_ids.wait()
    count_rows(1)
    give_src.wait()
    first_pass(1)

    for b in range(NX):
        block = rel_sum[b * LANES : (b + 1) * LANES, :].T
        for rows in range(NC):
            part[b, rows] = block[8 * rows : 8 * rows + 8, :]
    s1 = [
        remote(
            part.at[wrap(x + dx, NX), wrap(c + dc, NC)],
            part_in.at[n],
            s1_send.at[n],
            s1_recv.at[n],
            s1_peers[n],
        )
        for n, (dx, dc) in enumerate(s1_steps)
    ]
    for copy in s1:
        copy.start()

    second_pass(1)
    back_out[...] = src_sum[1].astype(BF16)
    back = remote(back_out, back_in, b_send.at[0], b_recv.at[0], ring[3])

    tile = part[x, c]
    for n, copy in enumerate(s1):
        copy.wait()
        tile = tile + part_in[n]
    mine[...] = tile

    s2 = [
        remote(mine, column.at[zh, zl, c], s2_send.at[n], s2_recv.at[n], s2_peer(step, far_y))
        for n, step in enumerate(s2_steps)
    ]
    for copy in s2[:0:-1]:
        copy.start()

    @pl.when(special)
    def _():
        s2[0].start()

    @pl.when(jnp.logical_not(special))
    def _():
        column[zh, zl, c] = mine[...]

    for copy in s2[1:]:
        copy.wait()

    @pl.when(special)
    def _():
        s2[0].wait()

    firsts = [column[0, l, 0] + column[1, l, 0] for l in range(ZL)]
    lasts = [column[0, l, 1] + column[1, l, 1] for l in range(ZL)]
    whole = [firsts[l] + lasts[(l + ZL - 1) % ZL] for l in range(ZL)]
    order = sorted(range(NY), key=lambda dy: (min(dy, NY - dy), dy))
    for n in range(2):
        full[x, 0, c, n] = jnp.where(c == 0, whole[n], whole[2 + n])
    s3 = [
        remote(full.at[x, 0, c], full.at[x, n, c], s3_send.at[n], s3_recv.at[n], s3_peers[order[n] - 1])
        for n in range(1, NY)
    ]
    for copy in s3[::-1]:
        copy.start()
    cuts = [0] + list(range(1, NY, 2)) + [NY]
    groups = [slice(a, b) for a, b in zip(cuts, cuts[1:])]

    def s4_copies(g):
        at = full.at[x, groups[g], c]
        return [remote(at, at, s4_send.at[g, n], s4_recv.at[g, n], s4_peers[n]) for n in range(NX - 1)]

    def s5_copy(g):
        at = full.at[:, groups[g], c]
        return remote(at, at, s5_send.at[g], s5_recv.at[g], sibling)

    s4 = [s4_copies(g) for g in range(len(groups))]
    s5 = [s5_copy(g) for g in range(len(groups))]
    for copy in s4[0]:
        copy.start()
    back.start()

    def update(total, table, acc, out, new_acc):
        accum = acc[...] + jnp.sum(total * total, axis=0, keepdims=True) * (1.0 / emb)
        new_acc[...] = accum
        out[...] = table[...] - total * (learn_rate / jnp.sqrt(accum))

    update(dst_sum[...], dest_emb, dest_acc, new_dest, new_dest_acc)

    def to_sibling(g):
        for copy in s4[g]:
            copy.wait_recv()
        s5[g].start()

    for g in range(1, len(groups)):
        for n in range(groups[g].start, groups[g].stop):
            s3[n - 1].wait_recv()
        for copy in s4[g]:
            copy.start()
        if g >= 2:
            to_sibling(g - 2)
    back.wait()
    update(src_sum[0] + back_in[...].astype(F32), source_emb, source_acc, new_source, new_source_acc)
    for g in range(max(0, len(groups) - 2), len(groups)):
        to_sibling(g)
    for copy in s5:
        copy.wait_recv()

    wide = min(LANES, rel_count)
    for h in range(rel_count // wide):
        at = slice(h * wide, (h + 1) * wide)
        tiles = []
        for b, (start, width) in enumerate(blocks):
            rows = []
            for t in range(wide // (8 * ZL)):
                steps = wrap(y + NY - (h * (wide // (8 * ZL)) + t), NY)
                spot = jnp.where(steps <= NY // 2, jnp.maximum(2 * steps - 1, 0), 2 * (NY - steps))
                rows.append(full[b, spot].reshape(8 * ZL, LANES))
            tiles.append(jnp.concatenate(rows, axis=0).T[:width])
        squares = sum(jnp.sum(tile * tile, axis=0, keepdims=True) for tile in tiles)
        accum = rel_acc[0:1, at] + squares * (1.0 / emb)
        new_rel_acc[0:1, at] = accum
        scale = learn_rate / jnp.sqrt(accum)
        for tile, (start, width) in zip(tiles, blocks):
            new_relations[start : start + width, at] = relations[start : start + width, at] - tile * scale

    for copy in s3:
        copy.wait_send()
    for g in range(len(groups)):
        for copy in s4[g]:
            copy.wait_send()
        s5[g].wait_send()


def write_out(*refs):
    count = (len(refs) - 1) // 2
    sem = refs[-1]
    copies = [pltpu.make_async_copy(refs[n], refs[count + n], sem.at[n]) for n in range(count)]
    for copy in copies:
        copy.start()
    for copy in copies:
        copy.wait()


def solution(mesh):
    n_src, n_dst = mesh.shape["src"], mesh.shape["dst"]
    NX, NY = n_src // (ZH * NC), n_dst // ZL

    def shards(
        source_emb,
        dest_emb,
        source_acc,
        dest_acc,
        relations,
        rel_acc,
        src_ids,
        dst_ids,
        rel_ids,
        neg_ids,
        counts,
    ):
        rows, emb = source_emb.shape
        rel_count = relations.shape[0]
        slots = src_ids.shape[3]
        chunks = pl.cdiv(slots, CHUNK)
        hbm = pl.BlockSpec(memory_space=pl.ANY)
        vmem = pl.BlockSpec(memory_space=pltpu.VMEM)
        dma = pltpu.SemaphoreType.DMA
        outs = pl.pallas_call(
            functools.partial(kernel, NX, NY),
            out_shape=(
                pltpu.VMEM((emb, rows), F32),
                pltpu.VMEM((emb, rows), F32),
                pltpu.VMEM((1, rows), F32),
                pltpu.VMEM((1, rows), F32),
                pltpu.VMEM((emb, rel_count), F32),
                pltpu.VMEM((1, rel_count), F32),
            ),
            in_specs=[hbm] * 11,
            out_specs=[vmem] * 6,
            scratch_shapes=[
                pltpu.SMEM((2,), jnp.int32),
                pltpu.VMEM((emb, rows), F32),
                pltpu.VMEM((emb, rows), F32),
                pltpu.VMEM((1, rows), F32),
                pltpu.VMEM((1, rows), F32),
                pltpu.VMEM((emb, rel_count), F32),
                pltpu.VMEM((1, rel_count), F32),
                pltpu.VMEM((2, slots), jnp.int32),
                pltpu.VMEM((2, slots), jnp.int32),
                pltpu.VMEM((2, slots), jnp.int32),
                pltpu.VMEM((2, slots), jnp.int32),
                pltpu.VMEM((3, chunks, 4, CHUNK), jnp.int32),
                pltpu.VMEM((2, emb, LANES), BF16),
                pltpu.VMEM((emb, LANES), BF16),
                pltpu.VMEM((LANES, emb), BF16),
                pltpu.VMEM((emb, LANES), BF16),
                pltpu.VMEM((2, LANES, CHUNK), F32),
                pltpu.VMEM((2 * chunks, 2, emb, CHUNK), BF16),
                pltpu.VMEM((2 * chunks, 3, LANES, CHUNK), BF16),
                pltpu.VMEM((2 * chunks, 2, emb, CHUNK), BF16),
                pltpu.VMEM((NX * LANES, LANES), F32),
                pltpu.VMEM((2, emb, LANES), F32),
                pltpu.VMEM((emb, LANES), F32),
                pltpu.VMEM((emb, LANES), BF16),
                pltpu.VMEM((emb, LANES), BF16),
                pltpu.VMEM((NX, NC, 8, LANES), F32),
                pltpu.VMEM((NX * NC - 1, 8, LANES), F32),
                pltpu.VMEM((8, LANES), F32),
                pltpu.VMEM((ZH, ZL, NC, 8, LANES), F32),
                pltpu.VMEM((NX, NY, NC, ZL // NC, 8, LANES), F32),
                dma((11,)),
                dma((2,)),
                dma((2,)),
                dma((1,)),
                dma((1,)),
                dma((NX * NC - 1,)),
                dma((NX * NC - 1,)),
                dma((ZH * ZL * NC,)),
                dma((ZH * ZL * NC,)),
                dma((NY,)),
                dma((NY,)),
                dma((NY, NX - 1)),
                dma((NY, NX - 1)),
                dma((NY,)),
                dma((NY,)),
            ],
            compiler_params=pltpu.CompilerParams(
                collective_id=0, has_side_effects=True, vmem_limit_bytes=40 * 2**20
            ),
            cost_estimate=pl.CostEstimate(flops=4 * 10**9, bytes_accessed=3 * 10**6, transcendentals=3 * 10**5),
            name="bucket_round",
        )(
            *(
                pltpu.with_memory_space_constraint(value, pltpu.HBM)
                for value in (
                    counts.reshape(2),
                    source_emb.T,
                    dest_emb.T,
                    source_acc.reshape(1, rows),
                    dest_acc.reshape(1, rows),
                    relations.T,
                    rel_acc.reshape(1, rel_count),
                    src_ids.reshape(2, slots),
                    dst_ids.reshape(2, slots),
                    rel_ids.reshape(2, slots),
                    neg_ids.reshape(2, slots),
                )
            )
        )
        outs = pl.pallas_call(
            write_out,
            out_shape=tuple(pltpu.HBM(out.shape, out.dtype) for out in outs),
            in_specs=[vmem] * 6,
            out_specs=[hbm] * 6,
            scratch_shapes=[dma((6,))],
            name="write_out",
        )(*(pltpu.with_memory_space_constraint(out, pltpu.VMEM) for out in outs))
        new_source, new_dest, new_source_acc, new_dest_acc, new_relations, new_rel_acc = outs
        return (
            new_source.T,
            new_dest.T,
            new_source_acc.reshape(rows),
            new_dest_acc.reshape(rows),
            new_relations.T,
            new_rel_acc.reshape(rel_count),
        )

    rows_spec = P(("src", "dst"), None)
    row_spec = P(("src", "dst"))
    ids_spec = P("src", "dst", None, None)
    return jax.shard_map(
        shards,
        mesh=mesh,
        in_specs=(rows_spec, rows_spec, row_spec, row_spec, P(), P())
        + (ids_spec,) * 4
        + (P("src", "dst", None),),
        out_specs=(rows_spec, rows_spec, row_spec, row_spec, P(), P()),
        check_vma=False,
    )
```

```python
import functools

import jax
import jax.numpy as jnp
from jax import lax
from jax.experimental import pallas as pl
from jax.experimental.pallas import tpu as pltpu
from jax.sharding import PartitionSpec as P

MESH = pl.DeviceIdType.MESH
F32 = jnp.float32
BF16 = jnp.bfloat16
learn_rate = 0.1

ZH, ZL, NC = 2, 4, 2
LANES = 128
CHUNK = 256
ABSENT = -1e30


def split2(value):
    high = value.astype(BF16)
    low = (value - high.astype(F32)).astype(BF16)
    return high, low


def nn(left, right):
    return jnp.dot(left, right, preferred_element_type=F32)


def nt(left, right):
    return lax.dot_general(left, right, (((1,), (1,)), ((), ())), preferred_element_type=F32)


def kernel(
    NX,
    NY,
    counts_hbm,
    source_emb_hbm,
    dest_emb_hbm,
    source_acc_hbm,
    dest_acc_hbm,
    relations_hbm,
    rel_acc_hbm,
    src_ids_hbm,
    dst_ids_hbm,
    rel_ids_hbm,
    neg_ids_hbm,
    new_source,
    new_dest,
    new_source_acc,
    new_dest_acc,
    new_relations,
    new_rel_acc,
    counts,
    source_emb,
    dest_emb,
    source_acc,
    dest_acc,
    relations,
    rel_acc,
    src_ids,
    dst_ids,
    rel_ids,
    neg_ids,
    ids,
    src_t,
    dst_t,
    dst_n,
    rel_t,
    count_b,
    query_s,
    weight_s,
    grad_s,
    rel_sum,
    src_sum,
    dst_sum,
    back_out,
    back_in,
    part,
    part_in,
    mine,
    column,
    full,
    in_sem,
    x_send,
    x_recv,
    b_send,
    b_recv,
    s1_send,
    s1_recv,
    s2_send,
    s2_recv,
    s3_send,
    s3_recv,
    s4_send,
    s4_recv,
    s5_send,
    s5_recv,
):
    loads = [
        pltpu.make_async_copy(src, dst, in_sem.at[n])
        for n, (src, dst) in enumerate(
            (
                (counts_hbm, counts),
                (rel_ids_hbm, rel_ids),
                (src_ids_hbm, src_ids),
                (dst_ids_hbm, dst_ids),
                (neg_ids_hbm, neg_ids),
                (source_emb_hbm, source_emb),
                (dest_emb_hbm, dest_emb),
                (relations_hbm, relations),
                (source_acc_hbm, source_acc),
                (dest_acc_hbm, dest_acc),
                (rel_acc_hbm, rel_acc),
            )
        )
    ]

    emb = source_emb.shape[0]
    half = emb // 2
    slots = src_ids.shape[1]
    chunks = pl.cdiv(slots, CHUNK)
    tail = slots - (chunks - 1) * CHUNK
    n_src, n_dst = NX * ZH * NC, NY * ZL
    rel_count = relations.shape[1]
    blocks = [(b * LANES, min(LANES, emb - b * LANES)) for b in range(NX)]

    i = lax.axis_index("src")
    j = lax.axis_index("dst")
    x, zh, c = i // (ZH * NC), jnp.bitwise_and(i // NC, ZH - 1), jnp.bitwise_and(i, NC - 1)
    y, zl = j // ZL, jnp.bitwise_and(j, ZL - 1)

    def place(x, zh, c, y, zl):
        return ((x * ZH + zh) * NC + c, y * ZL + zl)

    def wrap(value, size):
        return jnp.bitwise_and(value, size - 1)

    i_up, i_down = wrap(i + 1, n_src), wrap(i + n_src - 1, n_src)
    j_up, j_down = wrap(j + 1, n_dst), wrap(j + n_dst - 1, n_dst)
    ring = [(i_down, j), (i_up, j), (i_down, j_up), (i_up, j_down)]
    s1_steps = [(dx, dc) for dx in range(NX) for dc in range(NC) if dx or dc]
    s1_peers = [place(wrap(x + dx, NX), zh, wrap(c + dc, NC), y, zl) for dx, dc in s1_steps]
    s2_steps = [(dh, dl, dc) for dh in range(ZH) for dl in range(ZL) for dc in range(NC)]
    special = jnp.logical_and(zl == ZL - 1, c == 1)
    far_y = jnp.where(special, wrap(y + 1, NY), y)

    def s2_peer(step, at_y):
        dh, dl, dc = step
        return place(x, wrap(zh + dh, ZH), wrap(c + dc, NC), at_y, wrap(zl + dl, ZL))

    s3_peers = [place(x, zh, c, wrap(y + dy, NY), zl) for dy in range(1, NY)]
    s4_peers = [place(wrap(x + dx, NX), zh, c, y, zl) for dx in range(1, NX)]
    sibling = place(x, zh, 1 - c, y, zl)

    barrier = pltpu.get_barrier_semaphore()
    greeted = ring + s1_peers + s3_peers
    greeted += [s2_peer(step, y) for step in s2_steps[1:]]
    expected = len(greeted)
    before_y = wrap(y + NY - 1, NY)
    greeted += [place(x, h, 1, before_y, ZL - 1) for h in range(ZH)]
    for n, peer in enumerate(greeted):
        pl.semaphore_signal(barrier, inc=1, device_id=peer, device_id_type=MESH)
        if n == len(ring) - 1:
            for load in loads:
                load.start()

    def remote(src, dst, send, recv, peer):
        return pltpu.make_async_remote_copy(
            src_ref=src, dst_ref=dst, send_sem=send, recv_sem=recv, device_id=peer, device_id_type=MESH
        )

    lane = lax.broadcasted_iota(jnp.int32, (1, CHUNK), 1)
    for to in (0, 2):
        ids[to] = jnp.full(ids.shape[1:], -1, jnp.int32)
    for load in loads[:5]:
        load.wait()
    for s, to in ((1, 2), (0, 0)):
        live_count = counts[s]
        for n, table in enumerate((src_ids, dst_ids, rel_ids, neg_ids)):
            for q in range(chunks):
                width = CHUNK if q < chunks - 1 else tail
                row = table[s : s + 1, q * CHUNK : q * CHUNK + width]
                if n == 2:
                    row = jnp.bitwise_and(row - 8 * j, rel_count - 1)
                    row = jnp.where(lane[:, :width] + q * CHUNK < live_count, row, -1)
                ids[to, q, n : n + 1, 0:width] = row
    loads[5].wait()
    src_t[0] = source_emb[...].astype(BF16)

    pl.semaphore_wait(barrier, jnp.where(special, expected + ZH * ZL * NC, expected))
    give_ids = remote(ids.at[2], ids.at[1], x_send.at[0], x_recv.at[0], ring[0])
    give_src = remote(src_t.at[0], src_t.at[1], x_send.at[1], x_recv.at[1], ring[2])
    give_ids.start()
    give_src.start()
    for load in loads[6:]:
        load.wait()

    dst_t[...] = dest_emb[...].astype(BF16)
    for start, width in blocks:
        block = dest_emb[start : start + width, :]
        if width < LANES:
            block = jnp.concatenate([block, jnp.zeros((LANES - width, LANES), F32)], axis=0)
        dst_n[:, start : start + width] = block.T[:, :width].astype(BF16)

    row = lax.broadcasted_iota(jnp.int32, (rel_count, LANES), 0)
    spot = lax.broadcasted_iota(jnp.int32, (rel_count, LANES), 1)
    chosen = jnp.logical_and(row == jnp.bitwise_and(spot + 8 * j, rel_count - 1), spot < 16)
    rel_t[...] = nn(relations[...].astype(BF16), jnp.where(chosen, 1.0, 0.0).astype(BF16)).astype(BF16)

    iota = lax.broadcasted_iota(jnp.int32, (LANES, CHUNK), 0)

    def count_rows(s):
        seen = jnp.zeros((LANES, CHUNK), F32)
        for q in range(chunks):
            seen = seen + jnp.where(iota == ids[s, q, 3:4, :], 1.0, 0.0)
        count_b[s] = jnp.broadcast_to(jnp.sum(seen, axis=1, keepdims=True), (LANES, CHUNK))

    rel_sum[...] = jnp.zeros(rel_sum.shape, F32)
    src_sum[...] = jnp.zeros(src_sum.shape, F32)
    dst_sum[...] = jnp.zeros(dst_sum.shape, F32)

    def first_pass(s):
        def body(local, carry):
            q = s * chunks + local
            rows = ids[s, local]
            one_src = jnp.where(iota == rows[0:1], 1.0, 0.0).astype(BF16)
            hit_dst = iota == rows[1:2]
            one_rel = jnp.where(iota == rows[2:3], 1.0, 0.0).astype(BF16)
            a = nn(src_t[s], one_src)
            r = nn(rel_t[...], one_rel)
            a_re, a_im, r_re, r_im = a[:half], a[half:], r[:half], r[half:]
            query = jnp.concatenate([a_re * r_re - a_im * r_im, a_re * r_im + a_im * r_re], axis=0)
            query_high, query_low = split2(query)
            scores = nn(dst_n[...], query_high)
            rest = nn(dst_n[...], query_low)
            positive = jnp.sum(jnp.where(hit_dst, scores + rest, 0.0), axis=0, keepdims=True)
            seen = count_b[s]
            scores = jnp.where(seen > 0.0, scores, ABSENT)
            peak = jnp.maximum(jnp.max(scores, axis=0, keepdims=True), positive)
            pos_weight = jnp.exp(positive - peak)
            neg_weight = jnp.exp(scores - peak)
            partition = pos_weight + jnp.sum(neg_weight * seen, axis=0, keepdims=True)
            pos_coeff = pos_weight / partition - 1.0
            neg_coeff = (neg_weight * (1.0 / partition)).astype(BF16).astype(F32)
            pos_part = jnp.where(hit_dst, pos_coeff, 0.0)
            weight_high, weight_low = split2(neg_coeff * seen + pos_part)
            query_s[q, 0] = query_high
            query_s[q, 1] = query_low
            weight_s[q, 0] = weight_high
            weight_s[q, 1] = weight_low
            weight_s[q, 2] = pos_part.astype(BF16)
            table = dst_t[...]
            g = nn(
                jnp.concatenate([table, table], axis=1),
                jnp.concatenate([weight_high, weight_low], axis=0),
            )
            g_re, g_im = g[:half], g[half:]
            rel_grad = jnp.concatenate([g_re * a_re + g_im * a_im, g_im * a_re - g_re * a_im], axis=0)
            rel_high, rel_low = split2(rel_grad)
            rel_sum[0:emb, :] += nt(rel_high, one_rel) + nt(rel_low, one_rel)
            src_grad = jnp.concatenate([g_re * r_re + g_im * r_im, g_im * r_re - g_re * r_im], axis=0)
            src_high, src_low = split2(src_grad)
            grad_s[q, 0] = src_high
            grad_s[q, 1] = src_low
            return carry

        lax.fori_loop(0, chunks, body, 0, unroll=True)

    def second_pass(s):
        def body(local, carry):
            q = s * chunks + local
            rows = ids[s, local]
            one_src = jnp.where(iota == rows[0:1], 1.0, 0.0).astype(BF16)
            src_sum[s] += nt(grad_s[q, 0], one_src) + nt(grad_s[q, 1], one_src)
            dst_sum[...] += (
                nt(query_s[q, 0], weight_s[q, 0])
                + nt(query_s[q, 0], weight_s[q, 1])
                + nt(query_s[q, 1], weight_s[q, 2])
            )
            return carry

        lax.fori_loop(0, chunks, body, 0, unroll=True)

    count_rows(0)
    first_pass(0)
    second_pass(0)
    give_ids.wait()
    count_rows(1)
    give_src.wait()
    first_pass(1)

    for b in range(NX):
        block = rel_sum[b * LANES : (b + 1) * LANES, :].T
        for rows in range(NC):
            part[b, rows] = block[8 * rows : 8 * rows + 8, :]
    s1 = [
        remote(
            part.at[wrap(x + dx, NX), wrap(c + dc, NC)],
            part_in.at[n],
            s1_send.at[n],
            s1_recv.at[n],
            s1_peers[n],
        )
        for n, (dx, dc) in enumerate(s1_steps)
    ]
    for copy in s1:
        copy.start()

    second_pass(1)
    back_out[...] = src_sum[1].astype(BF16)
    back = remote(back_out, back_in, b_send.at[0], b_recv.at[0], ring[3])

    tile = part[x, c]
    for n, copy in enumerate(s1):
        copy.wait()
        tile = tile + part_in[n]
    mine[...] = tile

    s2 = [
        remote(mine, column.at[zh, zl, c], s2_send.at[n], s2_recv.at[n], s2_peer(step, far_y))
        for n, step in enumerate(s2_steps)
    ]
    for copy in s2[1:]:
        copy.start()

    @pl.when(special)
    def _():
        s2[0].start()

    @pl.when(jnp.logical_not(special))
    def _():
        column[zh, zl, c] = mine[...]

    for copy in s2[1:]:
        copy.wait()

    @pl.when(special)
    def _():
        s2[0].wait()

    firsts = [column[0, l, 0] + column[1, l, 0] for l in range(ZL)]
    lasts = [column[0, l, 1] + column[1, l, 1] for l in range(ZL)]
    whole = [firsts[l] + lasts[(l + ZL - 1) % ZL] for l in range(ZL)]
    order = sorted(range(NY), key=lambda dy: (min(dy, NY - dy), dy))
    for n in range(2):
        full[x, 0, c, n] = jnp.where(c == 0, whole[n], whole[2 + n])
    s3 = [
        remote(full.at[x, 0, c], full.at[x, n, c], s3_send.at[n], s3_recv.at[n], s3_peers[order[n] - 1])
        for n in range(1, NY)
    ]
    for copy in s3:
        copy.start()
    cuts = [0, 1, min(3, NY), min(5, NY), NY] if NY > 5 else [0, 1, NY]
    groups = [slice(a, b) for a, b in zip(cuts, cuts[1:])]

    def s4_copies(g):
        at = full.at[x, groups[g], c]
        return [remote(at, at, s4_send.at[g, n], s4_recv.at[g, n], s4_peers[n]) for n in range(NX - 1)]

    def s5_copy(g):
        at = full.at[:, groups[g], c]
        return remote(at, at, s5_send.at[g], s5_recv.at[g], sibling)

    s4 = [s4_copies(g) for g in range(len(groups))]
    s5 = [s5_copy(g) for g in range(len(groups))]
    for copy in s4[0]:
        copy.start()
    back.start()

    def update(total, table, acc, out, new_acc):
        accum = acc[...] + jnp.sum(total * total, axis=0, keepdims=True) * (1.0 / emb)
        new_acc[...] = accum
        out[...] = table[...] - total * (learn_rate / jnp.sqrt(accum))

    update(dst_sum[...], dest_emb, dest_acc, new_dest, new_dest_acc)

    def to_sibling(g):
        for copy in s4[g]:
            copy.wait_recv()
        s5[g].start()

    for g in range(1, len(groups)):
        for n in range(groups[g].start, groups[g].stop):
            s3[n - 1].wait_recv()
        for copy in s4[g]:
            copy.start()
        if g >= 2:
            to_sibling(g - 2)
    back.wait()
    update(src_sum[0] + back_in[...].astype(F32), source_emb, source_acc, new_source, new_source_acc)
    for g in range(max(0, len(groups) - 2), len(groups)):
        to_sibling(g)
    for copy in s5:
        copy.wait_recv()

    wide = min(LANES, rel_count)
    for h in range(rel_count // wide):
        at = slice(h * wide, (h + 1) * wide)
        tiles = []
        for b, (start, width) in enumerate(blocks):
            rows = []
            for t in range(wide // (8 * ZL)):
                steps = wrap(y + NY - (h * (wide // (8 * ZL)) + t), NY)
                spot = jnp.where(steps <= NY // 2, jnp.maximum(2 * steps - 1, 0), 2 * (NY - steps))
                rows.append(full[b, spot].reshape(8 * ZL, LANES))
            tiles.append(jnp.concatenate(rows, axis=0).T[:width])
        squares = sum(jnp.sum(tile * tile, axis=0, keepdims=True) for tile in tiles)
        accum = rel_acc[0:1, at] + squares * (1.0 / emb)
        new_rel_acc[0:1, at] = accum
        scale = learn_rate / jnp.sqrt(accum)
        for tile, (start, width) in zip(tiles, blocks):
            new_relations[start : start + width, at] = relations[start : start + width, at] - tile * scale

    for copy in s3:
        copy.wait_send()
    for g in range(len(groups)):
        for copy in s4[g]:
            copy.wait_send()
        s5[g].wait_send()


def write_out(*refs):
    count = (len(refs) - 1) // 2
    sem = refs[-1]
    copies = [pltpu.make_async_copy(refs[n], refs[count + n], sem.at[n]) for n in range(count)]
    for copy in copies:
        copy.start()
    for copy in copies:
        copy.wait()


def solution(mesh):
    n_src, n_dst = mesh.shape["src"], mesh.shape["dst"]
    NX, NY = n_src // (ZH * NC), n_dst // ZL

    def shards(
        source_emb,
        dest_emb,
        source_acc,
        dest_acc,
        relations,
        rel_acc,
        src_ids,
        dst_ids,
        rel_ids,
        neg_ids,
        counts,
    ):
        rows, emb = source_emb.shape
        rel_count = relations.shape[0]
        slots = src_ids.shape[3]
        chunks = pl.cdiv(slots, CHUNK)
        hbm = pl.BlockSpec(memory_space=pl.ANY)
        vmem = pl.BlockSpec(memory_space=pltpu.VMEM)
        dma = pltpu.SemaphoreType.DMA
        outs = pl.pallas_call(
            functools.partial(kernel, NX, NY),
            out_shape=(
                pltpu.VMEM((emb, rows), F32),
                pltpu.VMEM((emb, rows), F32),
                pltpu.VMEM((1, rows), F32),
                pltpu.VMEM((1, rows), F32),
                pltpu.VMEM((emb, rel_count), F32),
                pltpu.VMEM((1, rel_count), F32),
            ),
            in_specs=[hbm] * 11,
            out_specs=[vmem] * 6,
            scratch_shapes=[
                pltpu.SMEM((2,), jnp.int32),
                pltpu.VMEM((emb, rows), F32),
                pltpu.VMEM((emb, rows), F32),
                pltpu.VMEM((1, rows), F32),
                pltpu.VMEM((1, rows), F32),
                pltpu.VMEM((emb, rel_count), F32),
                pltpu.VMEM((1, rel_count), F32),
                pltpu.VMEM((2, slots), jnp.int32),
                pltpu.VMEM((2, slots), jnp.int32),
                pltpu.VMEM((2, slots), jnp.int32),
                pltpu.VMEM((2, slots), jnp.int32),
                pltpu.VMEM((3, chunks, 4, CHUNK), jnp.int32),
                pltpu.VMEM((2, emb, LANES), BF16),
                pltpu.VMEM((emb, LANES), BF16),
                pltpu.VMEM((LANES, emb), BF16),
                pltpu.VMEM((emb, LANES), BF16),
                pltpu.VMEM((2, LANES, CHUNK), F32),
                pltpu.VMEM((2 * chunks, 2, emb, CHUNK), BF16),
                pltpu.VMEM((2 * chunks, 3, LANES, CHUNK), BF16),
                pltpu.VMEM((2 * chunks, 2, emb, CHUNK), BF16),
                pltpu.VMEM((NX * LANES, LANES), F32),
                pltpu.VMEM((2, emb, LANES), F32),
                pltpu.VMEM((emb, LANES), F32),
                pltpu.VMEM((emb, LANES), BF16),
                pltpu.VMEM((emb, LANES), BF16),
                pltpu.VMEM((NX, NC, 8, LANES), F32),
                pltpu.VMEM((NX * NC - 1, 8, LANES), F32),
                pltpu.VMEM((8, LANES), F32),
                pltpu.VMEM((ZH, ZL, NC, 8, LANES), F32),
                pltpu.VMEM((NX, NY, NC, ZL // NC, 8, LANES), F32),
                dma((11,)),
                dma((2,)),
                dma((2,)),
                dma((1,)),
                dma((1,)),
                dma((NX * NC - 1,)),
                dma((NX * NC - 1,)),
                dma((ZH * ZL * NC,)),
                dma((ZH * ZL * NC,)),
                dma((NY,)),
                dma((NY,)),
                dma((NY, NX - 1)),
                dma((NY, NX - 1)),
                dma((NY,)),
                dma((NY,)),
            ],
            compiler_params=pltpu.CompilerParams(
                collective_id=0, has_side_effects=True, vmem_limit_bytes=40 * 2**20
            ),
            cost_estimate=pl.CostEstimate(flops=4 * 10**9, bytes_accessed=3 * 10**6, transcendentals=3 * 10**5),
            name="bucket_round",
        )(
            *(
                pltpu.with_memory_space_constraint(value, pltpu.HBM)
                for value in (
                    counts.reshape(2),
                    source_emb.T,
                    dest_emb.T,
                    source_acc.reshape(1, rows),
                    dest_acc.reshape(1, rows),
                    relations.T,
                    rel_acc.reshape(1, rel_count),
                    src_ids.reshape(2, slots),
                    dst_ids.reshape(2, slots),
                    rel_ids.reshape(2, slots),
                    neg_ids.reshape(2, slots),
                )
            )
        )
        outs = pl.pallas_call(
            write_out,
            out_shape=tuple(pltpu.HBM(out.shape, out.dtype) for out in outs),
            in_specs=[vmem] * 6,
            out_specs=[hbm] * 6,
            scratch_shapes=[dma((6,))],
            name="write_out",
        )(*(pltpu.with_memory_space_constraint(out, pltpu.VMEM) for out in outs))
        new_source, new_dest, new_source_acc, new_dest_acc, new_relations, new_rel_acc = outs
        return (
            new_source.T,
            new_dest.T,
            new_source_acc.reshape(rows),
            new_dest_acc.reshape(rows),
            new_relations.T,
            new_rel_acc.reshape(rel_count),
        )

    rows_spec = P(("src", "dst"), None)
    row_spec = P(("src", "dst"))
    ids_spec = P("src", "dst", None, None)
    return jax.shard_map(
        shards,
        mesh=mesh,
        in_specs=(rows_spec, rows_spec, row_spec, row_spec, P(), P())
        + (ids_spec,) * 4
        + (P("src", "dst", None),),
        out_specs=(rows_spec, rows_spec, row_spec, row_spec, P(), P()),
        check_vma=False,
    )
```

```python
import functools

import jax
import jax.numpy as jnp
from jax import lax
from jax.experimental import pallas as pl
from jax.experimental.pallas import tpu as pltpu
from jax.sharding import PartitionSpec as P

MESH = pl.DeviceIdType.MESH
F32 = jnp.float32
BF16 = jnp.bfloat16
learn_rate = 0.1

ZH, ZL, NC = 2, 4, 2
LANES = 128
CHUNK = 256
ABSENT = -1e30


def split2(value):
    high = value.astype(BF16)
    low = (value - high.astype(F32)).astype(BF16)
    return high, low


def nn(left, right):
    return jnp.dot(left, right, preferred_element_type=F32)


def nt(left, right):
    return lax.dot_general(left, right, (((1,), (1,)), ((), ())), preferred_element_type=F32)


def kernel(
    NX,
    NY,
    counts_hbm,
    source_emb_hbm,
    dest_emb_hbm,
    source_acc_hbm,
    dest_acc_hbm,
    relations_hbm,
    rel_acc_hbm,
    src_ids_hbm,
    dst_ids_hbm,
    rel_ids_hbm,
    neg_ids_hbm,
    new_source,
    new_dest,
    new_source_acc,
    new_dest_acc,
    new_relations,
    new_rel_acc,
    counts,
    source_emb,
    dest_emb,
    source_acc,
    dest_acc,
    relations,
    rel_acc,
    src_ids,
    dst_ids,
    rel_ids,
    neg_ids,
    ids,
    src_t,
    dst_t,
    dst_n,
    rel_t,
    count_b,
    query_s,
    weight_s,
    grad_s,
    rel_sum,
    src_sum,
    dst_sum,
    back_out,
    back_in,
    part,
    part_in,
    mine,
    column,
    full,
    in_sem,
    x_send,
    x_recv,
    b_send,
    b_recv,
    s1_send,
    s1_recv,
    s2_send,
    s2_recv,
    s3_send,
    s3_recv,
    s4_send,
    s4_recv,
    s5_send,
    s5_recv,
):
    loads = [
        pltpu.make_async_copy(src, dst, in_sem.at[n])
        for n, (src, dst) in enumerate(
            (
                (counts_hbm, counts),
                (rel_ids_hbm, rel_ids),
                (src_ids_hbm, src_ids),
                (dst_ids_hbm, dst_ids),
                (neg_ids_hbm, neg_ids),
                (source_emb_hbm, source_emb),
                (dest_emb_hbm, dest_emb),
                (relations_hbm, relations),
                (source_acc_hbm, source_acc),
                (dest_acc_hbm, dest_acc),
                (rel_acc_hbm, rel_acc),
            )
        )
    ]

    emb = source_emb.shape[0]
    half = emb // 2
    slots = src_ids.shape[1]
    chunks = pl.cdiv(slots, CHUNK)
    tail = slots - (chunks - 1) * CHUNK
    n_src, n_dst = NX * ZH * NC, NY * ZL
    rel_count = relations.shape[1]
    blocks = [(b * LANES, min(LANES, emb - b * LANES)) for b in range(NX)]

    i = lax.axis_index("src")
    j = lax.axis_index("dst")
    x, zh, c = i // (ZH * NC), jnp.bitwise_and(i // NC, ZH - 1), jnp.bitwise_and(i, NC - 1)
    y, zl = j // ZL, jnp.bitwise_and(j, ZL - 1)

    def place(x, zh, c, y, zl):
        return ((x * ZH + zh) * NC + c, y * ZL + zl)

    def wrap(value, size):
        return jnp.bitwise_and(value, size - 1)

    i_up, i_down = wrap(i + 1, n_src), wrap(i + n_src - 1, n_src)
    j_up, j_down = wrap(j + 1, n_dst), wrap(j + n_dst - 1, n_dst)
    ring = [(i_down, j), (i_up, j), (i_down, j_up), (i_up, j_down)]
    s1_steps = [(dx, dc) for dx in range(NX) for dc in range(NC) if dx or dc]
    s1_peers = [place(wrap(x + dx, NX), zh, wrap(c + dc, NC), y, zl) for dx, dc in s1_steps]
    s2_steps = [(dh, dl, dc) for dh in range(ZH) for dl in range(ZL) for dc in range(NC)]
    special = jnp.logical_and(zl == ZL - 1, c == 1)
    far_y = jnp.where(special, wrap(y + 1, NY), y)

    def s2_peer(step, at_y):
        dh, dl, dc = step
        return place(x, wrap(zh + dh, ZH), wrap(c + dc, NC), at_y, wrap(zl + dl, ZL))

    s3_peers = [place(x, zh, c, wrap(y + dy, NY), zl) for dy in range(1, NY)]
    s4_peers = [place(wrap(x + dx, NX), zh, c, y, zl) for dx in range(1, NX)]
    sibling = place(x, zh, 1 - c, y, zl)

    barrier = pltpu.get_barrier_semaphore()
    greeted = ring + s1_peers + s3_peers
    greeted += [s2_peer(step, y) for step in s2_steps[1:]]
    expected = len(greeted)
    before_y = wrap(y + NY - 1, NY)
    greeted += [place(x, h, 1, before_y, ZL - 1) for h in range(ZH)]
    for n, peer in enumerate(greeted):
        pl.semaphore_signal(barrier, inc=1, device_id=peer, device_id_type=MESH)
        if n == len(ring) - 1:
            for load in loads:
                load.start()

    def remote(src, dst, send, recv, peer):
        return pltpu.make_async_remote_copy(
            src_ref=src, dst_ref=dst, send_sem=send, recv_sem=recv, device_id=peer, device_id_type=MESH
        )

    lane = lax.broadcasted_iota(jnp.int32, (1, CHUNK), 1)
    for to in (0, 2):
        ids[to] = jnp.full(ids.shape[1:], -1, jnp.int32)
    for load in loads[:5]:
        load.wait()
    for s, to in ((1, 2), (0, 0)):
        live_count = counts[s]
        for n, table in enumerate((src_ids, dst_ids, rel_ids, neg_ids)):
            for q in range(chunks):
                width = CHUNK if q < chunks - 1 else tail
                row = table[s : s + 1, q * CHUNK : q * CHUNK + width]
                if n == 2:
                    row = jnp.bitwise_and(row - 8 * j, rel_count - 1)
                    row = jnp.where(lane[:, :width] + q * CHUNK < live_count, row, -1)
                ids[to, q, n : n + 1, 0:width] = row
    loads[5].wait()
    src_t[0] = source_emb[...].astype(BF16)

    pl.semaphore_wait(barrier, jnp.where(special, expected + ZH * ZL * NC, expected))
    give_ids = remote(ids.at[2], ids.at[1], x_send.at[0], x_recv.at[0], ring[0])
    give_src = remote(src_t.at[0], src_t.at[1], x_send.at[1], x_recv.at[1], ring[2])
    give_ids.start()
    give_src.start()
    for load in loads[6:]:
        load.wait()

    dst_t[...] = dest_emb[...].astype(BF16)
    for start, width in blocks:
        block = dest_emb[start : start + width, :]
        if width < LANES:
            block = jnp.concatenate([block, jnp.zeros((LANES - width, LANES), F32)], axis=0)
        dst_n[:, start : start + width] = block.T[:, :width].astype(BF16)

    row = lax.broadcasted_iota(jnp.int32, (rel_count, LANES), 0)
    spot = lax.broadcasted_iota(jnp.int32, (rel_count, LANES), 1)
    chosen = jnp.logical_and(row == jnp.bitwise_and(spot + 8 * j, rel_count - 1), spot < 16)
    rel_t[...] = nn(relations[...].astype(BF16), jnp.where(chosen, 1.0, 0.0).astype(BF16)).astype(BF16)

    iota = lax.broadcasted_iota(jnp.int32, (LANES, CHUNK), 0)

    def count_rows(s):
        seen = jnp.zeros((LANES, CHUNK), F32)
        for q in range(chunks):
            seen = seen + jnp.where(iota == ids[s, q, 3:4, :], 1.0, 0.0)
        count_b[s] = jnp.broadcast_to(jnp.sum(seen, axis=1, keepdims=True), (LANES, CHUNK))

    rel_sum[...] = jnp.zeros(rel_sum.shape, F32)
    src_sum[...] = jnp.zeros(src_sum.shape, F32)
    dst_sum[...] = jnp.zeros(dst_sum.shape, F32)

    def first_pass(s):
        def body(local, carry):
            q = s * chunks + local
            rows = ids[s, local]
            one_src = jnp.where(iota == rows[0:1], 1.0, 0.0).astype(BF16)
            hit_dst = iota == rows[1:2]
            one_rel = jnp.where(iota == rows[2:3], 1.0, 0.0).astype(BF16)
            a = nn(src_t[s], one_src)
            r = nn(rel_t[...], one_rel)
            a_re, a_im, r_re, r_im = a[:half], a[half:], r[:half], r[half:]
            query = jnp.concatenate([a_re * r_re - a_im * r_im, a_re * r_im + a_im * r_re], axis=0)
            query_high, query_low = split2(query)
            scores = nn(dst_n[...], query_high)
            rest = nn(dst_n[...], query_low)
            positive = jnp.sum(jnp.where(hit_dst, scores + rest, 0.0), axis=0, keepdims=True)
            seen = count_b[s]
            scores = jnp.where(seen > 0.0, scores, ABSENT)
            peak = jnp.maximum(jnp.max(scores, axis=0, keepdims=True), positive)
            pos_weight = jnp.exp(positive - peak)
            neg_weight = jnp.exp(scores - peak)
            partition = pos_weight + jnp.sum(neg_weight * seen, axis=0, keepdims=True)
            pos_coeff = pos_weight / partition - 1.0
            neg_coeff = (neg_weight * (1.0 / partition)).astype(BF16).astype(F32)
            pos_part = jnp.where(hit_dst, pos_coeff, 0.0)
            weight_high, weight_low = split2(neg_coeff * seen + pos_part)
            query_s[q, 0] = query_high
            query_s[q, 1] = query_low
            weight_s[q, 0] = weight_high
            weight_s[q, 1] = weight_low
            weight_s[q, 2] = pos_part.astype(BF16)
            table = dst_t[...]
            g = nn(
                jnp.concatenate([table, table], axis=1),
                jnp.concatenate([weight_high, weight_low], axis=0),
            )
            g_re, g_im = g[:half], g[half:]
            rel_grad = jnp.concatenate([g_re * a_re + g_im * a_im, g_im * a_re - g_re * a_im], axis=0)
            rel_high, rel_low = split2(rel_grad)
            rel_sum[0:emb, :] += nt(rel_high, one_rel) + nt(rel_low, one_rel)
            grad_s[q] = g
            return carry

        lax.fori_loop(0, chunks, body, 0, unroll=True)

    def second_pass(s):
        def body(local, carry):
            q = s * chunks + local
            rows = ids[s, local]
            one_src = jnp.where(iota == rows[0:1], 1.0, 0.0).astype(BF16)
            one_rel = jnp.where(iota == rows[2:3], 1.0, 0.0).astype(BF16)
            r = nn(rel_t[...], one_rel)
            g = grad_s[q]
            g_re, g_im, r_re, r_im = g[:half], g[half:], r[:half], r[half:]
            src_grad = jnp.concatenate([g_re * r_re + g_im * r_im, g_im * r_re - g_re * r_im], axis=0)
            src_high, src_low = split2(src_grad)
            src_sum[s] += nt(src_high, one_src) + nt(src_low, one_src)
            dst_sum[...] += (
                nt(query_s[q, 0], weight_s[q, 0])
                + nt(query_s[q, 0], weight_s[q, 1])
                + nt(query_s[q, 1], weight_s[q, 2])
            )
            return carry

        lax.fori_loop(0, chunks, body, 0, unroll=True)

    count_rows(0)
    first_pass(0)
    second_pass(0)
    give_ids.wait()
    count_rows(1)
    give_src.wait()
    first_pass(1)

    for b in range(NX):
        block = rel_sum[b * LANES : (b + 1) * LANES, :].T
        for rows in range(NC):
            part[b, rows] = block[8 * rows : 8 * rows + 8, :]
    s1 = [
        remote(
            part.at[wrap(x + dx, NX), wrap(c + dc, NC)],
            part_in.at[n],
            s1_send.at[n],
            s1_recv.at[n],
            s1_peers[n],
        )
        for n, (dx, dc) in enumerate(s1_steps)
    ]
    for copy in s1:
        copy.start()

    second_pass(1)
    back_out[...] = src_sum[1].astype(BF16)
    back = remote(back_out, back_in, b_send.at[0], b_recv.at[0], ring[3])

    tile = part[x, c]
    for n, copy in enumerate(s1):
        copy.wait()
        tile = tile + part_in[n]
    mine[...] = tile

    s2 = [
        remote(mine, column.at[zh, zl, c], s2_send.at[n], s2_recv.at[n], s2_peer(step, far_y))
        for n, step in enumerate(s2_steps)
    ]
    for copy in s2[1:]:
        copy.start()

    @pl.when(special)
    def _():
        s2[0].start()

    @pl.when(jnp.logical_not(special))
    def _():
        column[zh, zl, c] = mine[...]

    for copy in s2[1:]:
        copy.wait()

    @pl.when(special)
    def _():
        s2[0].wait()

    firsts = [column[0, l, 0] + column[1, l, 0] for l in range(ZL)]
    lasts = [column[0, l, 1] + column[1, l, 1] for l in range(ZL)]
    whole = [firsts[l] + lasts[(l + ZL - 1) % ZL] for l in range(ZL)]
    order = sorted(range(NY), key=lambda dy: (min(dy, NY - dy), dy))
    for n in range(2):
        full[x, 0, c, n] = jnp.where(c == 0, whole[n], whole[2 + n])
    s3 = [
        remote(full.at[x, 0, c], full.at[x, n, c], s3_send.at[n], s3_recv.at[n], s3_peers[order[n] - 1])
        for n in range(1, NY)
    ]
    for copy in s3:
        copy.start()
    cuts = [0, 1, min(3, NY), min(5, NY), NY] if NY > 5 else [0, 1, NY]
    groups = [slice(a, b) for a, b in zip(cuts, cuts[1:])]

    def s4_copies(g):
        at = full.at[x, groups[g], c]
        return [remote(at, at, s4_send.at[g, n], s4_recv.at[g, n], s4_peers[n]) for n in range(NX - 1)]

    def s5_copy(g):
        at = full.at[:, groups[g], c]
        return remote(at, at, s5_send.at[g], s5_recv.at[g], sibling)

    s4 = [s4_copies(g) for g in range(len(groups))]
    s5 = [s5_copy(g) for g in range(len(groups))]
    for copy in s4[0]:
        copy.start()
    back.start()

    def update(total, table, acc, out, new_acc):
        accum = acc[...] + jnp.sum(total * total, axis=0, keepdims=True) * (1.0 / emb)
        new_acc[...] = accum
        out[...] = table[...] - total * (learn_rate / jnp.sqrt(accum))

    update(dst_sum[...], dest_emb, dest_acc, new_dest, new_dest_acc)

    def to_sibling(g):
        for copy in s4[g]:
            copy.wait_recv()
        s5[g].start()

    for g in range(1, len(groups)):
        for n in range(groups[g].start, groups[g].stop):
            s3[n - 1].wait_recv()
        for copy in s4[g]:
            copy.start()
        if g >= 2:
            to_sibling(g - 2)
    back.wait()
    update(src_sum[0] + back_in[...].astype(F32), source_emb, source_acc, new_source, new_source_acc)
    for g in range(max(0, len(groups) - 2), len(groups)):
        to_sibling(g)
    for copy in s5:
        copy.wait_recv()

    wide = min(LANES, rel_count)
    for h in range(rel_count // wide):
        at = slice(h * wide, (h + 1) * wide)
        tiles = []
        for b, (start, width) in enumerate(blocks):
            rows = []
            for t in range(wide // (8 * ZL)):
                steps = wrap(y + NY - (h * (wide // (8 * ZL)) + t), NY)
                spot = jnp.where(steps <= NY // 2, jnp.maximum(2 * steps - 1, 0), 2 * (NY - steps))
                rows.append(full[b, spot].reshape(8 * ZL, LANES))
            tiles.append(jnp.concatenate(rows, axis=0).T[:width])
        squares = sum(jnp.sum(tile * tile, axis=0, keepdims=True) for tile in tiles)
        accum = rel_acc[0:1, at] + squares * (1.0 / emb)
        new_rel_acc[0:1, at] = accum
        scale = learn_rate / jnp.sqrt(accum)
        for tile, (start, width) in zip(tiles, blocks):
            new_relations[start : start + width, at] = relations[start : start + width, at] - tile * scale

    for copy in s3:
        copy.wait_send()
    for g in range(len(groups)):
        for copy in s4[g]:
            copy.wait_send()
        s5[g].wait_send()


def write_out(*refs):
    count = (len(refs) - 1) // 2
    sem = refs[-1]
    copies = [pltpu.make_async_copy(refs[n], refs[count + n], sem.at[n]) for n in range(count)]
    for copy in copies:
        copy.start()
    for copy in copies:
        copy.wait()


def solution(mesh):
    n_src, n_dst = mesh.shape["src"], mesh.shape["dst"]
    NX, NY = n_src // (ZH * NC), n_dst // ZL

    def shards(
        source_emb,
        dest_emb,
        source_acc,
        dest_acc,
        relations,
        rel_acc,
        src_ids,
        dst_ids,
        rel_ids,
        neg_ids,
        counts,
    ):
        rows, emb = source_emb.shape
        rel_count = relations.shape[0]
        slots = src_ids.shape[3]
        chunks = pl.cdiv(slots, CHUNK)
        hbm = pl.BlockSpec(memory_space=pl.ANY)
        vmem = pl.BlockSpec(memory_space=pltpu.VMEM)
        dma = pltpu.SemaphoreType.DMA
        outs = pl.pallas_call(
            functools.partial(kernel, NX, NY),
            out_shape=(
                pltpu.VMEM((emb, rows), F32),
                pltpu.VMEM((emb, rows), F32),
                pltpu.VMEM((1, rows), F32),
                pltpu.VMEM((1, rows), F32),
                pltpu.VMEM((emb, rel_count), F32),
                pltpu.VMEM((1, rel_count), F32),
            ),
            in_specs=[hbm] * 11,
            out_specs=[vmem] * 6,
            scratch_shapes=[
                pltpu.SMEM((2,), jnp.int32),
                pltpu.VMEM((emb, rows), F32),
                pltpu.VMEM((emb, rows), F32),
                pltpu.VMEM((1, rows), F32),
                pltpu.VMEM((1, rows), F32),
                pltpu.VMEM((emb, rel_count), F32),
                pltpu.VMEM((1, rel_count), F32),
                pltpu.VMEM((2, slots), jnp.int32),
                pltpu.VMEM((2, slots), jnp.int32),
                pltpu.VMEM((2, slots), jnp.int32),
                pltpu.VMEM((2, slots), jnp.int32),
                pltpu.VMEM((3, chunks, 4, CHUNK), jnp.int32),
                pltpu.VMEM((2, emb, LANES), BF16),
                pltpu.VMEM((emb, LANES), BF16),
                pltpu.VMEM((LANES, emb), BF16),
                pltpu.VMEM((emb, LANES), BF16),
                pltpu.VMEM((2, LANES, CHUNK), F32),
                pltpu.VMEM((2 * chunks, 2, emb, CHUNK), BF16),
                pltpu.VMEM((2 * chunks, 3, LANES, CHUNK), BF16),
                pltpu.VMEM((2 * chunks, emb, CHUNK), F32),
                pltpu.VMEM((NX * LANES, LANES), F32),
                pltpu.VMEM((2, emb, LANES), F32),
                pltpu.VMEM((emb, LANES), F32),
                pltpu.VMEM((emb, LANES), BF16),
                pltpu.VMEM((emb, LANES), BF16),
                pltpu.VMEM((NX, NC, 8, LANES), F32),
                pltpu.VMEM((NX * NC - 1, 8, LANES), F32),
                pltpu.VMEM((8, LANES), F32),
                pltpu.VMEM((ZH, ZL, NC, 8, LANES), F32),
                pltpu.VMEM((NX, NY, NC, ZL // NC, 8, LANES), F32),
                dma((11,)),
                dma((2,)),
                dma((2,)),
                dma((1,)),
                dma((1,)),
                dma((NX * NC - 1,)),
                dma((NX * NC - 1,)),
                dma((ZH * ZL * NC,)),
                dma((ZH * ZL * NC,)),
                dma((NY,)),
                dma((NY,)),
                dma((NY, NX - 1)),
                dma((NY, NX - 1)),
                dma((NY,)),
                dma((NY,)),
            ],
            compiler_params=pltpu.CompilerParams(
                collective_id=0, has_side_effects=True, vmem_limit_bytes=40 * 2**20
            ),
            cost_estimate=pl.CostEstimate(flops=4 * 10**9, bytes_accessed=3 * 10**6, transcendentals=3 * 10**5),
            name="bucket_round",
        )(
            *(
                pltpu.with_memory_space_constraint(value, pltpu.HBM)
                for value in (
                    counts.reshape(2),
                    source_emb.T,
                    dest_emb.T,
                    source_acc.reshape(1, rows),
                    dest_acc.reshape(1, rows),
                    relations.T,
                    rel_acc.reshape(1, rel_count),
                    src_ids.reshape(2, slots),
                    dst_ids.reshape(2, slots),
                    rel_ids.reshape(2, slots),
                    neg_ids.reshape(2, slots),
                )
            )
        )
        outs = pl.pallas_call(
            write_out,
            out_shape=tuple(pltpu.HBM(out.shape, out.dtype) for out in outs),
            in_specs=[vmem] * 6,
            out_specs=[hbm] * 6,
            scratch_shapes=[dma((6,))],
            name="write_out",
        )(*(pltpu.with_memory_space_constraint(out, pltpu.VMEM) for out in outs))
        new_source, new_dest, new_source_acc, new_dest_acc, new_relations, new_rel_acc = outs
        return (
            new_source.T,
            new_dest.T,
            new_source_acc.reshape(rows),
            new_dest_acc.reshape(rows),
            new_relations.T,
            new_rel_acc.reshape(rel_count),
        )

    rows_spec = P(("src", "dst"), None)
    row_spec = P(("src", "dst"))
    ids_spec = P("src", "dst", None, None)
    return jax.shard_map(
        shards,
        mesh=mesh,
        in_specs=(rows_spec, rows_spec, row_spec, row_spec, P(), P())
        + (ids_spec,) * 4
        + (P("src", "dst", None),),
        out_specs=(rows_spec, rows_spec, row_spec, row_spec, P(), P()),
        check_vma=False,
    )
```
